512 devices in a mesh: atm: 32 (over z_lo, y), ocn: 16 (over x, z_hi, core).
Axes of the slice: x: 4, y: 4, z: 16 (z_hi: 2, z_lo: 8; z = z_hi * 8 + z_lo), core: 2. Of those that a mesh axis runs over, the one named last changes fastest.
Arguments:
- atm_fields: float32 [16384, 16, 128], P(('atm', 'ocn')), may hold values from -6 to 6
- coupler_map: int32 [16, 1024], P('ocn'), may hold values from 0 to 1023, as said below
- remap_pattern: int32 [16384], P(('atm', 'ocn')), may hold values from 0 to 31, as said below
- remap_weights: float32 [16384, 128, 256], P(('atm', 'ocn')), may hold values from -0.375 to 0.375
- bulk_coeffs: float32 [4, 16], replicated, may hold values from -1.5 to 1.5
- ocean_state: float32 [4, 1024, 2048], P(None, 'atm', 'ocn'), may hold values from -6 to 6
- land_mask: int32 [1024, 2048], P('atm', 'ocn'), may hold values 0 or 1
Outputs:
- ocean_next: float32 [4, 1024, 2048], P(None, 'atm', 'ocn')
- atm_return: float32 [16384, 4, 128], P(('atm', 'ocn'))
The draws below stay inside these ranges and needn't reach their ends.
Inputs may be any that keep to these rules, and one draw needn't show every extreme that they name: `coupler_map`: each row is a permutation; of the 32 slots of one coupler device, exactly 1 come from each device of the same column. `remap_pattern`: the 32 entries of one device are a permutation of its local blocks.
All inputs are finite; a program needn't handle non-finite values. No bound on the sum of `land_mask` on one device may be relied on, other than what follows from the above.
Results may differ from the reference program's by a relative error of at most 0.00007.
Values sent between devices are 32-bit elements; how exact they have to be, the bound alone decides.
A program may use at most 64 MiB of HBM per device.

```python
import jax
import jax.numpy as jnp
from jax import lax

F = 16
NSTATE = 4
BS = 128
NNZ = 2
OROWS = 2
TY = 128
SUBSTEPS = 2
BLOCKS = 16384
OB = 256
NX = 1024
NY = 2048
N_ATM = 32
N_OCN = 16


def draw_coupler_map(key, part):
    key = jax.random.fold_in(key, 11)
    key_own, key_mix = jax.random.split(key)
    per_device = N_OCN * NNZ
    per_peer = per_device // N_ATM
    own_blocks = jax.vmap(lambda subkey: jax.random.permutation(subkey, per_device))(jax.random.split(key_own, N_OCN * N_ATM))
    own_blocks = own_blocks.reshape(N_OCN, N_ATM, N_ATM, per_peer).astype(jnp.int32)
    offset = (jnp.arange(N_ATM, dtype=jnp.int32) * per_device)[None, :, None, None]
    listed = jnp.transpose(own_blocks + offset, (0, 2, 1, 3)).reshape(N_OCN, N_ATM, per_device)
    shuffle = jax.vmap(lambda subkey: jax.random.permutation(subkey, per_device))(jax.random.split(key_mix, N_OCN * N_ATM))
    shuffle = shuffle.reshape(N_OCN, N_ATM, per_device)
    mixed = jnp.take_along_axis(listed, shuffle, axis=2)
    return mixed.reshape(N_OCN, N_ATM * per_device).astype(jnp.int32)


def draw_remap_pattern(key, part):
    key = jax.random.fold_in(key, 23)
    per_device = N_OCN * NNZ
    perms = jax.vmap(lambda subkey: jax.random.permutation(subkey, per_device))(jax.random.split(key, N_ATM * N_OCN))
    return perms.reshape(-1).astype(jnp.int32)


def plant(values, stream_key, least, high):
    spot = [jax.random.randint(jax.random.fold_in(stream_key, axis), (), 0, length) for axis, length in enumerate(values.shape)]
    widest = values.shape.index(max(values.shape))
    beside = spot[:widest] + [(spot[widest] + 1) % values.shape[widest]] + spot[widest + 1:]
    return values.at[tuple(spot)].set(least).at[tuple(beside)].set(high)


def steps_of(stream_key, extent, cuts, least, largest):
    gain, own = 1.0, jax.random.fold_in(stream_key, 6)
    for dim, parts in cuts:
        heights = jnp.exp(jax.random.uniform(jax.random.fold_in(own, dim), (parts,), jnp.float32, least / len(cuts), largest / len(cuts)))
        gain = gain * jnp.repeat(heights, extent[dim] // parts).reshape([-1 if axis == dim else 1 for axis in range(len(extent))])
    return gain


def centred(own_key, shape, width, most, pieces=(), kind=jnp.bfloat16):
    factor_of = steps_of(own_key, shape, pieces, -0.22, 0.18) if pieces else 1.0
    drawn = jax.random.normal(own_key, shape, jnp.float32) * width * factor_of
    return jnp.minimum(jnp.maximum(drawn, -most), most).astype(kind)


def setup_inputs(seed: int = 0) -> dict:
    splits = jax.random.split(jax.random.key(seed), 8)
    return {
        "atm_fields": centred(splits[0], (BLOCKS, F, BS), 1.0, 6.0, ((0, 512),), jnp.float32),
        "coupler_map": draw_coupler_map(jax.random.fold_in(splits[7], 71), 0),
        "remap_pattern": draw_remap_pattern(jax.random.fold_in(splits[7], 71), 0),
        "remap_weights": centred(splits[3], (BLOCKS, BS, OB), (NNZ * BS) ** -0.5, 0.375, ((0, 512),), jnp.float32),
        "bulk_coeffs": centred(splits[4], (NSTATE, F), F ** -0.5, 1.5, (), jnp.float32),
        "ocean_state": centred(splits[5], (NSTATE, NX, NY), 1.0, 6.0, ((1, 32), (2, 16)), jnp.float32),
        "land_mask": plant((jax.random.randint(splits[6], (NX, NY), 0, 4) < 3).astype(jnp.int32), jax.random.fold_in(splits[6], 1), 0, 1),
    }


def advance(ocean_now, padded, forcing, wet_cells):
    laplace = padded[:, 2:, 1:-1] + padded[:, :-2, 1:-1] + padded[:, 1:-1, 2:] + padded[:, 1:-1, :-2] - 4.0 * ocean_now
    zero_field = jnp.zeros_like(ocean_now[0])
    rotation = jnp.stack([ocean_now[1], -ocean_now[0], zero_field, zero_field])
    kappa = jnp.array([0.8, 0.8, 0.5, 0.5], jnp.float32)[:, None, None]
    tendency = kappa * laplace + 0.5 * rotation - 0.1 * ocean_now + forcing
    return wet_cells * (ocean_now + 0.25 * tendency)


def reference(atm_fields, coupler_map, remap_pattern, remap_weights, bulk_coeffs, ocean_state, land_mask):
    highest = lax.Precision.HIGHEST
    per_device = N_OCN * NNZ
    fields = atm_fields.reshape(N_ATM, N_OCN, per_device, F, BS).transpose(1, 0, 2, 3, 4)
    fields = fields.reshape(N_OCN, N_ATM * per_device, F, BS)
    columns = jax.vmap(lambda column, indices: column[indices])(fields, coupler_map)
    coupled = columns.reshape(N_OCN, N_ATM, per_device, F, BS).transpose(1, 0, 2, 3, 4)
    pattern = remap_pattern.reshape(N_ATM, N_OCN, per_device)
    gathered = jax.vmap(jax.vmap(lambda blocks, indices: blocks[indices]))(coupled, pattern)
    gathered = gathered.reshape(N_ATM, N_OCN, N_OCN, NNZ, F, BS)
    weights = remap_weights.reshape(N_ATM, N_OCN, N_OCN, NNZ, BS, OB)
    fluxes = jnp.einsum('aodkfb,aodkbq->aofdq', gathered, weights, precision=highest)
    fluxes = fluxes.reshape(N_ATM, N_OCN, F, N_OCN, OROWS, TY).transpose(2, 0, 1, 4, 3, 5).reshape(F, NX, NY)
    forcing = jnp.einsum('sf,fxy->sxy', bulk_coeffs, fluxes, precision=highest)
    wet_cells = land_mask.astype(jnp.float32)
    ocean_now = ocean_state
    for substep in range(SUBSTEPS):
        padded = jnp.pad(ocean_now, ((0, 0), (1, 1), (1, 1)))
        ocean_now = advance(ocean_now, padded, forcing, wet_cells)
    sampled = ocean_now.reshape(NSTATE, N_ATM, N_OCN, OROWS, N_OCN, TY).transpose(1, 2, 0, 4, 3, 5)
    sampled = sampled.reshape(N_ATM, N_OCN, NSTATE, N_OCN, OB)
    back_terms = jnp.einsum('aocdq,aodkbq->aodkcb', sampled, weights, precision=highest)
    back_terms = back_terms.reshape(N_ATM, N_OCN, per_device, NSTATE, BS)
    returned = jax.vmap(jax.vmap(lambda terms, indices: jnp.zeros_like(terms).at[indices].add(terms)))(back_terms, pattern)
    return ocean_now, returned.reshape(BLOCKS, NSTATE, BS)
```

```python
import functools

import jax
import jax.numpy as jnp
from jax import lax
from jax.experimental import pallas as pl
from jax.experimental.pallas import tpu as pltpu
from jax.sharding import PartitionSpec as P

MESH = pl.DeviceIdType.MESH
F32 = jnp.float32
BF16 = jnp.bfloat16
NSTATE = 4
F = 16
C = 128
HIGHEST = lax.Precision.HIGHEST


def iota(shape, dim):
    return lax.broadcasted_iota(jnp.int32, shape, dim)


def split(x):
    high = x.astype(BF16).astype(F32)
    return jnp.concatenate([high, x - high], axis=0).astype(BF16)


def tend(x, lap, mask, state):
    rows = x.shape[0]
    rot = jnp.where(
        state == 0,
        pltpu.roll(x, rows - 1, 0),
        jnp.where(state == 1, -pltpu.roll(x, 1, 0), 0.0),
    )
    kappa = jnp.where(state < 2, F32(0.8), F32(0.5))
    return mask * (x + 0.25 * (kappa * lap + 0.5 * rot - 0.1 * x))


def kernel(
    na, no,
    atm_h, w_h, st_h, mk_h, cm_v, cm_s, pat_s, c_v,
    on_h, ar_h,
    atm, w32, whi, wlo, st, mk,
    out1, arr1, idx_s,
    row_out, row_in, col_out, col_in,
    mask_out, mask_in, a2_out, a2_in,
    g, g_up, g_dn, on_out, on_in, on_t, back, ar,
    in_sem, w_sem, x_send, x_recv, row_send, row_recv, col_send, col_recv, g_send, g_recv, out_sem,
):
    nb = na
    r4 = NSTATE * nb
    a = lax.axis_index("atm")
    o = lax.axis_index("ocn")
    line = a * no + o

    st_copy = pltpu.make_async_copy(st_h, st, in_sem.at[0])
    mk_copy = pltpu.make_async_copy(mk_h, mk, in_sem.at[1])
    atm_copy = pltpu.make_async_copy(atm_h, atm, in_sem.at[2])
    atm_copy.start()
    st_copy.start()
    mk_copy.start()
    for d in range(no):
        pltpu.make_async_copy(w_h.at[d], w32.at[d], w_sem.at[d]).start()

    barrier = pltpu.get_barrier_semaphore()

    def greet_atm(k, carry):
        pl.semaphore_signal(barrier, inc=1, device_id=(lax.rem(a + k, na), o), device_id_type=MESH)
        return carry

    def greet_ocn(k, carry):
        pl.semaphore_signal(barrier, inc=1, device_id=(a, lax.rem(o + k, no)), device_id_type=MESH)
        return carry

    lax.fori_loop(1, na, greet_atm, 0)
    lax.fori_loop(1, no, greet_ocn, 0)
    cross_up = jnp.logical_and(o == 0, a > 0)
    cross_dn = jnp.logical_and(o == no - 1, a < na - 1)

    @pl.when(cross_up)
    def _():
        pl.semaphore_signal(barrier, inc=1, device_id=(a - 1, no - 1), device_id_type=MESH)

    @pl.when(cross_dn)
    def _():
        pl.semaphore_signal(barrier, inc=1, device_id=(a + 1, 0), device_id_type=MESH)

    slot = iota((r4, na * nb), 1)
    cm = cm_v[...]
    mine = jnp.where(cm // nb == a, (cm % nb).astype(F32), 0.0)
    mine = jnp.where(slot // nb == iota((r4, na * nb), 0) // NSTATE, mine, 0.0)
    order = jnp.sum(mine, axis=1, keepdims=True).astype(jnp.int32)
    coeff = c_v[...]
    coeff = jnp.concatenate([coeff] * 2, axis=0)
    coeff = jnp.concatenate([coeff] * (C // F), axis=1)
    coeff = jnp.concatenate([coeff] * (r4 // 8), axis=0)
    coeff = jnp.concatenate([coeff] * (nb * F // C), axis=1)
    take = jnp.where(order == iota((r4, nb * F), 1) // F, coeff, 0.0)
    atm_copy.wait()
    states = jnp.dot(take, atm[...], precision=HIGHEST, preferred_element_type=F32)
    for b in range(nb):
        out1[b] = states[NSTATE * b : NSTATE * b + NSTATE]
    arr1[a] = out1[a]

    st_copy.wait()
    mk_copy.wait()
    land = mk[...].astype(F32)
    for b in range(no):
        mask_out[b] = land[2 * b : 2 * b + 2]
    mask_in[o] = mask_out[o]
    for s in range(NSTATE):
        a2_out[pl.ds(s, nb, stride=NSTATE), :] = land
    wet = a2_out[...]
    for s in range(NSTATE):
        a2_out[pl.ds(s, nb, stride=NSTATE), :] = st[s]
    tile = a2_out[...]
    state = iota((r4, C), 0) % NSTATE
    lane = iota((r4, C), 1)

    def edges(rnd, x):
        row_out[rnd, 0] = x[:NSTATE]
        row_out[rnd, 1] = x[r4 - NSTATE :]
        turned = x.T
        col_out[rnd, 0] = turned[:1]
        col_out[rnd, 1] = turned[C - 1 :]

    def halo_copies(rnd):
        def row(side, target):
            return pltpu.make_async_remote_copy(
                row_out.at[rnd, side], row_in.at[rnd, 1 - side], row_send.at[rnd, side], row_recv.at[rnd, 1 - side],
                device_id=(target, o), device_id_type=MESH)

        def col(side, target):
            return pltpu.make_async_remote_copy(
                col_out.at[rnd, side], col_in.at[rnd, 1 - side], col_send.at[rnd, side], col_recv.at[rnd, 1 - side],
                device_id=(a, target), device_id_type=MESH)

        return (
            (a > 0, row(0, a - 1)),
            (a < na - 1, row(1, a + 1)),
            (o > 0, col(0, o - 1)),
            (o < no - 1, col(1, o + 1)),
        )

    def start_halo(rnd):
        for there, copy in halo_copies(rnd):
            @pl.when(there)
            def _():
                copy.start()

    def wait_halo_send(rnd):
        for there, copy in halo_copies(rnd):
            @pl.when(there)
            def _():
                copy.wait_send()

    def wait_halo_recv(rnd):
        for side, there, neighbour in ((0, a > 0, a - 1), (1, a < na - 1, a + 1)):
            @pl.when(there)
            def _():
                pltpu.make_async_remote_copy(
                    row_out.at[rnd, side], row_in.at[rnd, side], row_send.at[rnd, side], row_recv.at[rnd, side],
                    device_id=(neighbour, o), device_id_type=MESH).wait_recv()
        for side, there, neighbour in ((0, o > 0, o - 1), (1, o < no - 1, o + 1)):
            @pl.when(there)
            def _():
                pltpu.make_async_remote_copy(
                    col_out.at[rnd, side], col_in.at[rnd, side], col_send.at[rnd, side], col_recv.at[rnd, side],
                    device_id=(a, neighbour), device_id_type=MESH).wait_recv()

    for side, outside in ((0, a == 0), (1, a == na - 1)):
        @pl.when(outside)
        def _():
            row_in[0, side] = jnp.zeros((NSTATE, C), F32)
            row_in[1, side] = jnp.zeros((NSTATE, C), F32)

    for side, outside in ((0, o == 0), (1, o == no - 1)):
        @pl.when(outside)
        def _():
            col_in[0, side] = jnp.zeros((1, r4), F32)
            col_in[1, side] = jnp.zeros((1, r4), F32)

    @pl.when(line == 0)
    def _():
        g_up[...] = jnp.zeros_like(g_up)

    @pl.when(line == na * no - 1)
    def _():
        g_dn[...] = jnp.zeros_like(g_dn)

    def substep(rnd, x):
        up = jnp.concatenate([row_in[rnd, 0], x[: r4 - NSTATE]], axis=0)
        down = jnp.concatenate([x[NSTATE:], row_in[rnd, 1]], axis=0)
        at = iota((C, r4), 0)
        beside = jnp.where(at == 0, col_in[rnd, 0], jnp.where(at == C - 1, col_in[rnd, 1], 0.0)).T
        left = jnp.where(lane == 0, beside, pltpu.roll(x, 1, 1))
        right = jnp.where(lane == C - 1, beside, pltpu.roll(x, C - 1, 1))
        return tend(x, up + down + left + right - 4.0 * x, wet, state)

    edges(0, tile)
    pl.semaphore_wait(barrier, na + no - 2 + cross_up.astype(jnp.int32) + cross_dn.astype(jnp.int32))

    def send_block(k, carry):
        to = lax.rem(a + k, na)
        pltpu.make_async_remote_copy(
            out1.at[to], arr1.at[a], x_send.at[0], x_recv.at[0], device_id=(to, o), device_id_type=MESH).start()
        return carry

    lax.fori_loop(1, na, send_block, 0)
    start_halo(0)

    def send_mask(k, carry):
        to = lax.rem(o + k, no)
        pltpu.make_async_remote_copy(
            mask_out.at[to], mask_in.at[o], x_send.at[1], x_recv.at[1], device_id=(a, to), device_id_type=MESH).start()
        return carry

    lax.fori_loop(1, no, send_mask, 0)

    for r in range(nb):
        idx_s[r] = cm_s[0, a * nb + pat_s[r]] // nb

    def split_weights(d, carry):
        pltpu.make_async_copy(w_h.at[d], w32.at[d], w_sem.at[d]).wait()
        w = w32[d]
        high = w.astype(BF16)
        whi[d] = high
        wlo[d] = (w - high.astype(F32)).astype(BF16)
        return carry

    lax.fori_loop(0, no, split_weights, 0)

    wait_halo_recv(0)
    tile = substep(0, tile)
    edges(1, tile)
    start_halo(1)
    wait_halo_recv(1)
    a2_out[...] = substep(1, tile)

    def rows_of(d):
        return pl.ds(pl.multiple_of(8 * d, 8), 8)

    a2_in[rows_of(o)] = a2_out[rows_of(o)]

    def send_a2(k, carry):
        to = lax.rem(o + k, no)
        pltpu.make_async_remote_copy(
            a2_out.at[rows_of(to)], a2_in.at[rows_of(o)], x_send.at[2], x_recv.at[2],
            device_id=(a, to), device_id_type=MESH).start()
        return carry

    lax.fori_loop(1, no, send_a2, 0)

    def wait_all(i, ref, count, send):
        part = ref.at[pl.ds(0, count)]
        copy = pltpu.make_async_remote_copy(
            part, part, x_send.at[i], x_recv.at[i], device_id=(a, o), device_id_type=MESH)
        if send:
            copy.wait_send()
        else:
            copy.wait_recv()

    wait_all(1, mask_in, no - 1, False)
    wait_all(0, arr1, nb - 1, False)
    for d in range(no):
        x = jnp.concatenate([arr1[idx_s[2 * d]], arr1[idx_s[2 * d + 1]]], axis=1)
        x = split(x)
        f = jnp.dot(x, whi[d], preferred_element_type=F32) + jnp.dot(x, wlo[d], preferred_element_type=F32)
        f = 0.25 * (f[:NSTATE] + f[NSTATE:])
        g[0, d] = f[:, :C] * mask_in[d, 0:1]
        g[1, d] = f[:, C:] * mask_in[d, 1:2]

    above = ((line - 1) // no, (line - 1) % no)
    below = ((line + 1) // no, (line + 1) % no)

    @pl.when(line > 0)
    def _():
        pltpu.make_async_remote_copy(
            g.at[0], g_dn, g_send.at[0], g_recv.at[1], device_id=above, device_id_type=MESH).start()

    @pl.when(line < na * no - 1)
    def _():
        pltpu.make_async_remote_copy(
            g.at[1], g_up, g_send.at[1], g_recv.at[0], device_id=below, device_id_type=MESH).start()

    wait_all(2, a2_in, 8 * (no - 1), False)

    @pl.when(line > 0)
    def _():
        pltpu.make_async_remote_copy(
            g.at[0], g_up, g_send.at[0], g_recv.at[0], device_id=above, device_id_type=MESH).wait_recv()

    @pl.when(line < na * no - 1)
    def _():
        pltpu.make_async_remote_copy(
            g.at[1], g_dn, g_send.at[1], g_recv.at[1], device_id=below, device_id_type=MESH).wait_recv()

    state8 = iota((8, C), 0) % NSTATE
    lane8 = iota((8, C), 1)
    rows = [jnp.concatenate([g[0, d], g[1, d]], axis=0) for d in range(no)]
    lefts = [pltpu.roll(x, 1, 1) for x in rows]
    rights = [pltpu.roll(x, C - 1, 1) for x in rows]
    nothing = jnp.zeros((8, C), F32)
    for d in range(no):
        x = rows[d]
        up = jnp.concatenate([g_up[d], x[:NSTATE]], axis=0)
        down = jnp.concatenate([x[NSTATE:], g_dn[d]], axis=0)
        left = jnp.where(lane8 == 0, lefts[d - 1] if d > 0 else nothing, lefts[d])
        right = jnp.where(lane8 == C - 1, rights[d + 1] if d < no - 1 else nothing, rights[d])
        wet8 = jnp.where(iota((8, C), 0) < NSTATE, mask_in[d, 0:1], mask_in[d, 1:2])
        on_out[8 * d : 8 * d + 8] = a2_in[8 * d : 8 * d + 8] + (x + tend(x, up + down + left + right - 4.0 * x, wet8, state8))

    on_in[rows_of(o)] = on_out[rows_of(o)]

    def send_on(k, carry):
        to = lax.rem(o + k, no)
        pltpu.make_async_remote_copy(
            on_out.at[rows_of(to)], on_in.at[rows_of(o)], x_send.at[3], x_recv.at[3],
            device_id=(a, to), device_id_type=MESH).start()
        return carry

    lax.fori_loop(1, no, send_on, 0)

    nt = (((1,), (1,)), ((), ()))
    for d in range(no):
        x = on_out[8 * d : 8 * d + 8]
        x = split(jnp.concatenate([x[:NSTATE], x[NSTATE:]], axis=1))
        f = lax.dot_general(x, whi[d], nt, preferred_element_type=F32) + lax.dot_general(
            x, wlo[d], nt, preferred_element_type=F32)
        f = f[:NSTATE] + f[NSTATE:]
        back[8 * d : 8 * d + 8] = jnp.concatenate([f[:, :C], f[:, C:]], axis=0)

    across = iota((r4, r4), 1)
    along = iota((r4, r4), 0)
    pattern = jnp.zeros((1, r4), jnp.int32)
    for r in range(nb):
        pattern = jnp.where(iota((1, r4), 1) // NSTATE == r, pat_s[r], pattern)
    place = jnp.logical_and(pattern == along // NSTATE, across % NSTATE == along % NSTATE)
    placed = jnp.dot(jnp.where(place, 1.0, 0.0).astype(F32), back[...], precision=HIGHEST, preferred_element_type=F32)
    for b in range(nb):
        ar[b] = placed[NSTATE * b : NSTATE * b + NSTATE]
    ar_copy = pltpu.make_async_copy(ar, ar_h, out_sem.at[0])
    ar_copy.start()

    wait_all(3, on_in, 8 * (no - 1), False)
    for s in range(NSTATE):
        on_t[s] = on_in[pl.ds(s, nb, stride=NSTATE), :]
    on_copy = pltpu.make_async_copy(on_t, on_h, out_sem.at[1])
    on_copy.start()

    wait_all(0, out1, nb - 1, True)
    wait_all(1, mask_out, no - 1, True)
    wait_all(2, a2_out, 8 * (no - 1), True)
    wait_all(3, on_out, 8 * (no - 1), True)
    wait_halo_send(0)
    wait_halo_send(1)

    @pl.when(line > 0)
    def _():
        pltpu.make_async_remote_copy(
            g.at[0], g_dn, g_send.at[0], g_recv.at[1], device_id=above, device_id_type=MESH).wait_send()

    @pl.when(line < na * no - 1)
    def _():
        pltpu.make_async_remote_copy(
            g.at[1], g_up, g_send.at[1], g_recv.at[0], device_id=below, device_id_type=MESH).wait_send()

    ar_copy.wait()
    on_copy.wait()


def body(na, no, atm_fields, coupler_map, remap_pattern, remap_weights, bulk_coeffs, ocean_state, land_mask):
    nb = atm_fields.shape[0]
    r4 = NSTATE * nb
    any_space = pl.BlockSpec(memory_space=pl.ANY)
    vmem = pl.BlockSpec(memory_space=pltpu.VMEM)
    smem = pl.BlockSpec(memory_space=pltpu.SMEM)
    dma = pltpu.SemaphoreType.DMA
    return pl.pallas_call(
        functools.partial(kernel, na, no),
        out_shape=(
            jax.ShapeDtypeStruct(ocean_state.shape, F32),
            jax.ShapeDtypeStruct((nb, NSTATE, C), F32),
        ),
        in_specs=[any_space, any_space, any_space, any_space, vmem, smem, smem, vmem],
        out_specs=(any_space, any_space),
        scratch_shapes=[
            pltpu.VMEM((nb * F, C), F32),
            pltpu.VMEM((no, 2 * C, 2 * C), F32),
            pltpu.VMEM((no, 2 * C, 2 * C), BF16),
            pltpu.VMEM((no, 2 * C, 2 * C), BF16),
            pltpu.VMEM((NSTATE, nb, C), F32),
            pltpu.VMEM((nb, C), jnp.int32),
            pltpu.VMEM((nb, NSTATE, C), F32),
            pltpu.VMEM((nb, NSTATE, C), F32),
            pltpu.SMEM((nb,), jnp.int32),
            pltpu.VMEM((2, 2, NSTATE, C), F32),
            pltpu.VMEM((2, 2, NSTATE, C), F32),
            pltpu.VMEM((2, 2, 1, r4), F32),
            pltpu.VMEM((2, 2, 1, r4), F32),
            pltpu.VMEM((no, 2, C), F32),
            pltpu.VMEM((no, 2, C), F32),
            pltpu.VMEM((r4, C), F32),
            pltpu.VMEM((r4, C), F32),
            pltpu.VMEM((2, no, NSTATE, C), F32),
            pltpu.VMEM((no, NSTATE, C), F32),
            pltpu.VMEM((no, NSTATE, C), F32),
            pltpu.VMEM((r4, C), F32),
            pltpu.VMEM((r4, C), F32),
            pltpu.VMEM((NSTATE, nb, C), F32),
            pltpu.VMEM((r4, C), F32),
            pltpu.VMEM((nb, NSTATE, C), F32),
            dma((3,)),
            dma((no,)),
            dma((4,)),
            dma((4,)),
            dma((2, 2)),
            dma((2, 2)),
            dma((2, 2)),
            dma((2, 2)),
            dma((2,)),
            dma((2,)),
            dma((2,)),
        ],
        compiler_params=pltpu.CompilerParams(
            collective_id=0, has_side_effects=True, vmem_limit_bytes=32 * 1024 * 1024
        ),
    )(
        atm_fields.reshape(nb * F, C),
        remap_weights.reshape(no, 2 * C, 2 * C),
        ocean_state,
        land_mask,
        coupler_map,
        coupler_map,
        remap_pattern,
        bulk_coeffs,
    )


def solution(mesh):
    in_specs = (
        P(("atm", "ocn"), None, None),
        P("ocn", None),
        P(("atm", "ocn")),
        P(("atm", "ocn"), None, None),
        P(),
        P(None, "atm", "ocn"),
        P("atm", "ocn"),
    )
    out_specs = (P(None, "atm", "ocn"), P(("atm", "ocn"), None, None))
    step = functools.partial(body, mesh.shape["atm"], mesh.shape["ocn"])
    return jax.shard_map(step, mesh=mesh, in_specs=in_specs, out_specs=out_specs, check_vma=False)
```

```python
import functools

import jax
import jax.numpy as jnp
from jax import lax
from jax.experimental import pallas as pl
from jax.experimental.pallas import tpu as pltpu
from jax.sharding import PartitionSpec as P

MESH = pl.DeviceIdType.MESH
F32 = jnp.float32
BF16 = jnp.bfloat16
NSTATE = 4
F = 16
C = 128
HIGHEST = lax.Precision.HIGHEST


def iota(shape, dim):
    return lax.broadcasted_iota(jnp.int32, shape, dim)


def split(x):
    high = x.astype(BF16).astype(F32)
    return jnp.concatenate([high, x - high], axis=0).astype(BF16)


def tend(x, lap, mask, state):
    rows = x.shape[0]
    rot = jnp.where(
        state == 0,
        pltpu.roll(x, rows - 1, 0),
        jnp.where(state == 1, -pltpu.roll(x, 1, 0), 0.0),
    )
    kappa = jnp.where(state < 2, F32(0.8), F32(0.5))
    return mask * (x + 0.25 * (kappa * lap + 0.5 * rot - 0.1 * x))


def kernel(
    na, no,
    atm_h, w_h, st_h, mk_h, cm_h, pat_h, c_h,
    on_h, ar_h,
    cm_v, cm_s, pat_s, c_v,
    atm, w32, whi, wlo, st, mk,
    out1, arr1, idx_s,
    row_out, row_in, col_out, col_in,
    mask_out, mask_in, a2_out, a2_in,
    g, g_up, g_dn, gx, g_in, edge_out, edge_in, g_halo, on_t, back, ar,
    in_sem, w_sem, x_send, x_recv, row_send, row_recv, col_send, col_recv, g_send, g_recv, h_send, h_recv, out_sem,
):
    nb = na
    r4 = NSTATE * nb
    a = lax.axis_index("atm")
    o = lax.axis_index("ocn")
    line = a * no + o

    nz = na // 4
    half = (a // 4) // (nz // 2)
    nx = no // 4

    def atm_peer(k):
        i = k // 4
        return (i * half + (nz - 1 - i) * (1 - half)) * 4 + k % 4

    def ocn_peer(k):
        rest = k % (no // 2)
        x = (o // 4 + rest // 2 + nx // 2) % nx
        z = (o // 2 + 1 + k // (no // 2)) % 2
        return x * 4 + z * 2 + (o + rest) % 2

    def each(count, peer, me, act):
        def step(k, carry):
            to = peer(k)

            @pl.when(to != me)
            def _():
                act(to)

            return carry

        lax.fori_loop(0, count, step, 0)

    barrier = pltpu.get_barrier_semaphore()

    def greet(device):
        pl.semaphore_signal(barrier, inc=1, device_id=device, device_id_type=MESH)

    each(no, ocn_peer, o, lambda to: greet((a, to)))
    each(na, atm_peer, a, lambda to: greet((to, o)))
    has_up, has_dn, has_left, has_right = a > 0, a < na - 1, o > 0, o < no - 1
    corners = []
    for dv, vert in ((-1, has_up), (1, has_dn)):
        @pl.when(vert)
        def _():
            greet((a + dv, no - 1 if dv < 0 else 0))

        for dh, hori in ((-1, has_left), (1, has_right)):
            corners.append((dv, dh, jnp.logical_and(vert, hori)))

            @pl.when(corners[-1][2])
            def _():
                greet((a + dv, o + dh))

    first = jnp.logical_and(o == 0, has_up)
    last = jnp.logical_and(o == no - 1, has_dn)
    greetings = na + no - 2 + no * (first.astype(jnp.int32) + last.astype(jnp.int32))
    for _, _, there in corners:
        greetings += there.astype(jnp.int32)

    copies = [
        pltpu.make_async_copy(src, dst, in_sem.at[i])
        for i, (src, dst) in enumerate((
            (cm_h, cm_v), (c_h, c_v), (atm_h, atm), (st_h, st), (mk_h, mk), (cm_h, cm_s), (pat_h, pat_s)))
    ]
    for copy in copies:
        copy.start()
    for d in range(no):
        pltpu.make_async_copy(w_h.at[d], w32.at[d], w_sem.at[d]).start()

    copies[0].wait()
    copies[1].wait()
    slot = iota((r4, na * nb), 1)
    cm = cm_v[...]
    mine = jnp.where(cm // nb == a, (cm % nb).astype(F32), 0.0)
    mine = jnp.where(slot // nb == iota((r4, na * nb), 0) // NSTATE, mine, 0.0)
    order = jnp.sum(mine, axis=1, keepdims=True).astype(jnp.int32)
    coeff = c_v[...]
    coeff = jnp.concatenate([coeff] * 2, axis=0)
    coeff = jnp.concatenate([coeff] * (C // F), axis=1)
    coeff = jnp.concatenate([coeff] * (r4 // 8), axis=0)
    coeff = jnp.concatenate([coeff] * (nb * F // C), axis=1)
    take = jnp.where(order == iota((r4, nb * F), 1) // F, coeff, 0.0)
    copies[2].wait()
    states = jnp.dot(take, atm[...], precision=HIGHEST, preferred_element_type=F32)
    for b in range(nb):
        out1[b] = states[NSTATE * b : NSTATE * b + NSTATE]
    arr1[a] = out1[a]

    copies[3].wait()
    copies[4].wait()
    land = mk[...].astype(F32)
    for b in range(no):
        mask_out[b] = land[2 * b : 2 * b + 2]
    mask_in[o] = mask_out[o]
    for s in range(NSTATE):
        a2_out[pl.ds(s, nb, stride=NSTATE), :] = land
    wet = a2_out[...]
    for s in range(NSTATE):
        a2_out[pl.ds(s, nb, stride=NSTATE), :] = st[s]
    tile = a2_out[...]
    turned, wet_turned = tile.T, wet.T
    for i in range(2):
        row_out[0, i] = tile[NSTATE * i : NSTATE * i + NSTATE]
        row_out[1, i] = tile[r4 - NSTATE * i - NSTATE : r4 - NSTATE * i]
        col_out[0, i : i + 1] = turned[i : i + 1]
        col_out[1, i : i + 1] = turned[C - 1 - i : C - i]
    row_out[0, 2] = wet[:NSTATE]
    row_out[1, 2] = wet[r4 - NSTATE :]
    col_out[0, 2:3] = wet_turned[:1]
    col_out[1, 2:3] = wet_turned[C - 1 :]
    for side in range(2):
        col_out[side, 3:4] = jnp.zeros((1, r4), F32)

    def row_copy(side, up_or_down, target):
        return pltpu.make_async_remote_copy(
            row_out.at[side], row_in.at[up_or_down], row_send.at[side], row_recv.at[up_or_down],
            device_id=(target, o), device_id_type=MESH)

    def col_copy(side, place, flight, target):
        return pltpu.make_async_remote_copy(
            col_out.at[side], col_in.at[place], col_send.at[flight], col_recv.at[place],
            device_id=target, device_id_type=MESH)

    halos = [
        (has_left, col_copy(0, 3, 2, (a, o - 1)), col_copy(0, 2, 2, (a, o - 1))),
        (has_right, col_copy(1, 2, 3, (a, o + 1)), col_copy(1, 3, 3, (a, o + 1))),
    ]
    for dv, dh, there in corners:
        side = 0 if dh < 0 else 1
        here = (0 if dv < 0 else 4) + side
        halos.append((there, col_copy(side, 5 - here, here, (a + dv, o + dh)), col_copy(side, here, here, (a + dv, o + dh))))
    halos.append((has_up, row_copy(0, 1, a - 1), row_copy(0, 0, a - 1)))
    halos.append((has_dn, row_copy(1, 0, a + 1), row_copy(1, 1, a + 1)))

    for side, inside in ((0, has_up), (1, has_dn)):
        @pl.when(jnp.logical_not(inside))
        def _():
            row_in[side] = jnp.zeros((3, NSTATE, C), F32)
            g_halo[side] = jnp.zeros((NSTATE, C), F32)

    places = [(2, has_left), (3, has_right)]
    places += [((0 if dv < 0 else 4) + (0 if dh < 0 else 1), there) for dv, dh, there in corners]
    for place, inside in places:
        @pl.when(jnp.logical_not(inside))
        def _():
            col_in[place] = jnp.zeros((4, r4), F32)

    has_above, has_below = line > 0, line < na * no - 1

    @pl.when(jnp.logical_not(has_above))
    def _():
        g_up[...] = jnp.zeros_like(g_up)

    @pl.when(jnp.logical_not(has_below))
    def _():
        g_dn[...] = jnp.zeros_like(g_dn)

    def block_copy(to):
        return pltpu.make_async_remote_copy(
            out1.at[to], arr1.at[a], x_send.at[0], x_recv.at[0], device_id=(to, o), device_id_type=MESH)

    def ocn_copy(i, src, dst, to):
        return pltpu.make_async_remote_copy(
            src, dst, x_send.at[i], x_recv.at[i], device_id=(a, to), device_id_type=MESH)

    def rows_of(d):
        return pl.ds(pl.multiple_of(8 * d, 8), 8)

    pl.semaphore_wait(barrier, greetings)
    each(na, atm_peer, a, lambda to: block_copy(to).start())
    for there, copy, _ in halos:
        @pl.when(there)
        def _():
            copy.start()

    each(no, ocn_peer, o, lambda to: ocn_copy(1, mask_out.at[to], mask_in.at[o], to).start())

    copies[5].wait()
    copies[6].wait()
    for r in range(nb):
        idx_s[r] = cm_s[0, a * nb + pat_s[r]] // nb

    def split_weights(d, carry):
        pltpu.make_async_copy(w_h.at[d], w32.at[d], w_sem.at[d]).wait()
        w = w32[d]
        high = w.astype(BF16)
        whi[d] = high
        wlo[d] = (w - high.astype(F32)).astype(BF16)
        return carry

    lax.fori_loop(0, no, split_weights, 0)
    across = iota((r4, r4), 1)
    along = iota((r4, r4), 0)
    pattern = jnp.zeros((1, r4), jnp.int32)
    for r in range(nb):
        pattern = jnp.where(iota((1, r4), 1) // NSTATE == r, pat_s[r], pattern)
    place = jnp.logical_and(pattern == along // NSTATE, across % NSTATE == along % NSTATE)
    place = jnp.where(place, 1.0, 0.0).astype(F32)

    for there, _, copy in halos:
        @pl.when(there)
        def _():
            copy.wait_recv()

    at, along_lane = iota((C, r4), 0), iota((C, r4), 1)
    beside = jnp.zeros((C, r4), F32)
    for i in range(3):
        beside = jnp.where(at == i, col_in[3, i : i + 1], beside)
        beside = jnp.where(at == C - 1 - i, col_in[2, i : i + 1], beside)
    diagonal = jnp.where(
        at == 0,
        jnp.where(along_lane < r4 // 2, col_in[5, :1], col_in[1, :1]),
        jnp.where(at == C - 1, jnp.where(along_lane < r4 // 2, col_in[4, :1], col_in[0, :1]), 0.0))
    beside, diagonal = beside.T, diagonal.T
    rows = r4 + 4 * NSTATE
    lane = iota((rows, C), 1)
    state = iota((rows, C), 0) % NSTATE
    none = jnp.zeros((NSTATE, C), F32)
    x = jnp.concatenate([row_in[0, 1], row_in[0, 0], tile, row_in[1, 0], row_in[1, 1]], axis=0)
    e = jnp.concatenate([none, diagonal[r4 - NSTATE :], beside, diagonal[:NSTATE], none], axis=0)
    wet_x = jnp.concatenate([none, row_in[0, 2], wet, row_in[1, 2], none], axis=0)
    wet_e = jnp.concatenate([none, none, beside, none, none], axis=0)
    wet_e = jnp.where(lane == 0, pltpu.roll(wet_e, C - 2, 1), jnp.where(lane == C - 1, pltpu.roll(wet_e, 2, 1), 0.0))

    def sides(x, e):
        x_right, e_right = pltpu.roll(x, 1, 1), pltpu.roll(e, 1, 1)
        x_left, e_left = pltpu.roll(x, C - 1, 1), pltpu.roll(e, C - 1, 1)
        low, high = iota(x.shape, 1) == 0, iota(x.shape, 1) == C - 1
        of_x = jnp.where(low, e_right, x_right) + jnp.where(high, e_left, x_left)
        of_e = jnp.where(low, x_right, e_right) + jnp.where(high, x_left, e_left)
        return of_x, of_e

    def rises(x):
        return pltpu.roll(x, NSTATE, 0) + pltpu.roll(x, rows - NSTATE, 0)

    of_x, of_e = sides(x, e)
    x, e = tend(x, rises(x) + of_x - 4.0 * x, wet_x, state), tend(e, rises(e) + of_e - 4.0 * e, wet_e, state)
    of_x, _ = sides(x, e)
    x = tend(x, rises(x) + of_x - 4.0 * x, wet_x, state)
    a2_out[...] = x[2 * NSTATE : 2 * NSTATE + r4]
    a2_in[rows_of(o)] = a2_out[rows_of(o)]
    each(no, ocn_peer, o, lambda to: ocn_copy(2, a2_out.at[rows_of(to)], a2_in.at[rows_of(o)], to).start())

    def wait_all(i, ref, count, send):
        part = ref.at[pl.ds(0, count)]
        copy = ocn_copy(i, part, part, o)
        if send:
            copy.wait_send()
        else:
            copy.wait_recv()

    wait_all(1, mask_in, no - 1, False)
    wait_all(0, arr1, nb - 1, False)
    pairs = []
    for d in range(no):
        x = jnp.concatenate([arr1[idx_s[2 * d]], arr1[idx_s[2 * d + 1]]], axis=1)
        x = split(x)
        f = jnp.dot(x, whi[d], preferred_element_type=F32) + jnp.dot(x, wlo[d], preferred_element_type=F32)
        f = 0.25 * (f[:NSTATE] + f[NSTATE:])
        upper, lower = f[:, :C] * mask_in[d, 0:1], f[:, C:] * mask_in[d, 1:2]
        g[0, d] = upper
        g[1, d] = lower
        pairs.append(jnp.concatenate([upper, lower], axis=0))
        gx[8 * d : 8 * d + 8] = pairs[d]

        @pl.when(o != d)
        def _():
            ocn_copy(3, gx.at[pl.ds(8 * d, 8)], g_in.at[rows_of(o)], d).start()

    g_in[rows_of(o)] = gx[rows_of(o)]
    above = ((line - 1) // no, (line - 1) % no)
    below = ((line + 1) // no, (line + 1) % no)

    def g_copy(row, dst, place, target):
        return pltpu.make_async_remote_copy(
            g.at[row], dst, g_send.at[row], g_recv.at[place], device_id=target, device_id_type=MESH)

    @pl.when(has_above)
    def _():
        g_copy(0, g_dn, 1, above).start()

    @pl.when(has_below)
    def _():
        g_copy(1, g_up, 0, below).start()

    lane8, row8 = iota((8, C), 1), iota((8, C), 0)
    nothing = jnp.zeros((8, C), F32)
    lefts = [pltpu.roll(x, 1, 1) for x in pairs]
    rights = [pltpu.roll(x, C - 1, 1) for x in pairs]
    for d in range(no):
        before = pairs[d - 1][:, C - 1 :] if d > 0 else jnp.zeros((8, 1), F32)
        after = pairs[d + 1][:, :1] if d < no - 1 else jnp.zeros((8, 1), F32)
        both = jnp.where(lane8 == row8, before, jnp.where(lane8 == row8 + 8, after, 0.0))
        edge_out[d] = jnp.sum(both, axis=0, keepdims=True)

        @pl.when(o != d)
        def _():
            ocn_copy(4, edge_out.at[d], edge_in.at[o], d).start()

    edge_in[o] = edge_out[o]

    def halo_copy(row, d, target):
        return pltpu.make_async_remote_copy(
            g.at[row, d], g_halo.at[1 - row], h_send.at[row], h_recv.at[1 - row],
            device_id=(target, d), device_id_type=MESH)

    @pl.when(first)
    def _():
        for d in range(no):
            halo_copy(0, d, a - 1).start()

    @pl.when(last)
    def _():
        for d in range(no):
            halo_copy(1, d, a + 1).start()

    wait_all(2, a2_in, 8 * (no - 1), False)

    @pl.when(has_above)
    def _():
        g_copy(0, g_up, 0, above).wait_recv()

    @pl.when(has_below)
    def _():
        g_copy(1, g_dn, 1, below).wait_recv()

    nt = (((1,), (1,)), ((), ()))
    for d in range(no):
        x = pairs[d]
        up = jnp.concatenate([g_up[d], x[:NSTATE]], axis=0)
        down = jnp.concatenate([x[NSTATE:], g_dn[d]], axis=0)
        left = jnp.where(lane8 == 0, lefts[d - 1] if d > 0 else nothing, lefts[d])
        right = jnp.where(lane8 == C - 1, rights[d + 1] if d < no - 1 else nothing, rights[d])
        wet8 = jnp.where(row8 < NSTATE, mask_in[d, 0:1], mask_in[d, 1:2])
        x = a2_in[8 * d : 8 * d + 8] + (x + tend(x, up + down + left + right - 4.0 * x, wet8, row8 % NSTATE))
        x = split(jnp.concatenate([x[:NSTATE], x[NSTATE:]], axis=1))
        f = lax.dot_general(x, whi[d], nt, preferred_element_type=F32) + lax.dot_general(
            x, wlo[d], nt, preferred_element_type=F32)
        f = f[:NSTATE] + f[NSTATE:]
        back[8 * d : 8 * d + 8] = jnp.concatenate([f[:, :C], f[:, C:]], axis=0)

    placed = jnp.dot(place, back[...], precision=HIGHEST, preferred_element_type=F32)
    for b in range(nb):
        ar[b] = placed[NSTATE * b : NSTATE * b + NSTATE]
    ar_copy = pltpu.make_async_copy(ar, ar_h, out_sem.at[0])
    ar_copy.start()

    wait_all(3, g_in, 8 * (no - 1), False)
    wait_all(4, edge_in, no - 1, False)

    @pl.when(has_up)
    def _():
        halo_copy(1, 0, a).wait_recv()

    @pl.when(has_dn)
    def _():
        halo_copy(0, 0, a).wait_recv()

    x = g_in[...]
    edge = jnp.concatenate([jnp.broadcast_to(edge_in[b], (8, C)) for b in range(no)], axis=0)
    lane, row = iota((r4, C), 1), iota((r4, C), 0)
    before = jnp.sum(jnp.where(lane == row % 8, edge, 0.0), axis=1, keepdims=True)
    after = jnp.sum(jnp.where(lane == row % 8 + 8, edge, 0.0), axis=1, keepdims=True)
    up = jnp.concatenate([g_halo[0], x[: r4 - NSTATE]], axis=0)
    down = jnp.concatenate([x[NSTATE:], g_halo[1]], axis=0)
    left = jnp.where(lane == 0, before, pltpu.roll(x, 1, 1))
    right = jnp.where(lane == C - 1, after, pltpu.roll(x, C - 1, 1))
    g_in[...] = a2_out[...] + (x + tend(x, up + down + left + right - 4.0 * x, wet, row % NSTATE))
    for s in range(NSTATE):
        on_t[s] = g_in[pl.ds(s, nb, stride=NSTATE), :]
    on_copy = pltpu.make_async_copy(on_t, on_h, out_sem.at[1])
    on_copy.start()

    wait_all(0, out1, nb - 1, True)
    wait_all(1, mask_out, no - 1, True)
    wait_all(2, a2_out, 8 * (no - 1), True)
    wait_all(3, gx, 8 * (no - 1), True)
    wait_all(4, edge_out, no - 1, True)
    for there, copy, _ in halos:
        @pl.when(there)
        def _():
            copy.wait_send()

    @pl.when(has_above)
    def _():
        g_copy(0, g_dn, 1, above).wait_send()

    @pl.when(has_below)
    def _():
        g_copy(1, g_up, 0, below).wait_send()

    for row, sends in ((0, first), (1, last)):
        @pl.when(sends)
        def _():
            pltpu.make_async_remote_copy(
                g.at[row], g_up, h_send.at[row], h_recv.at[1 - row], device_id=(a, o), device_id_type=MESH).wait_send()

    ar_copy.wait()
    on_copy.wait()


def body(na, no, atm_fields, coupler_map, remap_pattern, remap_weights, bulk_coeffs, ocean_state, land_mask):
    nb = atm_fields.shape[0]
    r4 = NSTATE * nb
    any_space = pl.BlockSpec(memory_space=pl.ANY)
    dma = pltpu.SemaphoreType.DMA
    return pl.pallas_call(
        functools.partial(kernel, na, no),
        out_shape=(
            jax.ShapeDtypeStruct(ocean_state.shape, F32),
            jax.ShapeDtypeStruct((nb, NSTATE, C), F32),
        ),
        in_specs=[any_space] * 7,
        out_specs=(any_space, any_space),
        scratch_shapes=[
            pltpu.VMEM((1, na * nb), jnp.int32),
            pltpu.SMEM((1, na * nb), jnp.int32),
            pltpu.SMEM((nb,), jnp.int32),
            pltpu.VMEM((NSTATE, F), F32),
            pltpu.VMEM((nb * F, C), F32),
            pltpu.VMEM((no, 2 * C, 2 * C), F32),
            pltpu.VMEM((no, 2 * C, 2 * C), BF16),
            pltpu.VMEM((no, 2 * C, 2 * C), BF16),
            pltpu.VMEM((NSTATE, nb, C), F32),
            pltpu.VMEM((nb, C), jnp.int32),
            pltpu.VMEM((nb, NSTATE, C), F32),
            pltpu.VMEM((nb, NSTATE, C), F32),
            pltpu.SMEM((nb,), jnp.int32),
            pltpu.VMEM((2, 3, NSTATE, C), F32),
            pltpu.VMEM((2, 3, NSTATE, C), F32),
            pltpu.VMEM((2, 4, r4), F32),
            pltpu.VMEM((6, 4, r4), F32),
            pltpu.VMEM((no, 2, C), F32),
            pltpu.VMEM((no, 2, C), F32),
            pltpu.VMEM((r4, C), F32),
            pltpu.VMEM((r4, C), F32),
            pltpu.VMEM((2, no, NSTATE, C), F32),
            pltpu.VMEM((no, NSTATE, C), F32),
            pltpu.VMEM((no, NSTATE, C), F32),
            pltpu.VMEM((r4, C), F32),
            pltpu.VMEM((r4, C), F32),
            pltpu.VMEM((no, 1, C), F32),
            pltpu.VMEM((no, 1, C), F32),
            pltpu.VMEM((2, NSTATE, C), F32),
            pltpu.VMEM((NSTATE, nb, C), F32),
            pltpu.VMEM((r4, C), F32),
            pltpu.VMEM((nb, NSTATE, C), F32),
            dma((7,)),
            dma((no,)),
            dma((5,)),
            dma((5,)),
            dma((2,)),
            dma((2,)),
            dma((6,)),
            dma((6,)),
            dma((2,)),
            dma((2,)),
            dma((2,)),
            dma((2,)),
            dma((2,)),
        ],
        compiler_params=pltpu.CompilerParams(
            collective_id=0, has_side_effects=True, vmem_limit_bytes=63 * 1024 * 1024
        ),
    )(
        atm_fields.reshape(nb * F, C),
        remap_weights.reshape(no, 2 * C, 2 * C),
        ocean_state,
        land_mask,
        coupler_map,
        remap_pattern,
        bulk_coeffs,
    )


def solution(mesh):
    in_specs = (
        P(("atm", "ocn"), None, None),
        P("ocn", None),
        P(("atm", "ocn")),
        P(("atm", "ocn"), None, None),
        P(),
        P(None, "atm", "ocn"),
        P("atm", "ocn"),
    )
    out_specs = (P(None, "atm", "ocn"), P(("atm", "ocn"), None, None))
    step = functools.partial(body, mesh.shape["atm"], mesh.shape["ocn"])
    return jax.shard_map(step, mesh=mesh, in_specs=in_specs, out_specs=out_specs, check_vma=False)
```

```python
import functools

import jax
import jax.numpy as jnp
from jax import lax
from jax.experimental import pallas as pl
from jax.experimental.pallas import tpu as pltpu
from jax.sharding import PartitionSpec as P

MESH = pl.DeviceIdType.MESH
F32 = jnp.float32
BF16 = jnp.bfloat16
NSTATE = 4
F = 16
C = 128
HIGHEST = lax.Precision.HIGHEST


def iota(shape, dim):
    return lax.broadcasted_iota(jnp.int32, shape, dim)


def split(x):
    high = x.astype(BF16).astype(F32)
    return jnp.concatenate([high, x - high], axis=0).astype(BF16)


def tend(x, lap, mask, state):
    rows = x.shape[0]
    rot = jnp.where(
        state == 0,
        pltpu.roll(x, rows - 1, 0),
        jnp.where(state == 1, -pltpu.roll(x, 1, 0), 0.0),
    )
    kappa = jnp.where(state < 2, F32(0.8), F32(0.5))
    return mask * (x + 0.25 * (kappa * lap + 0.5 * rot - 0.1 * x))


def kernel(
    na, no,
    atm_h, w_h, st_h, mk_h, cm_h, pat_h, c_h,
    flat, back,
    cm_v, cm_s, pat_s, c_v,
    atm, w32, whi, wlo, st, mk,
    out1, arr1, idx_s,
    row_out, row_in, col_out, col_in,
    mask_out, mask_in, a2_out, a2_in, a2_part, fix_out, fix_in,
    g, g_up, g_dn, gx, g_in, edge_out, edge_in, g_halo,
    in_sem, w_sem, x_send, x_recv, row_send, row_recv, col_send, col_recv, g_send, g_recv, h_send, h_recv,
):
    nb = na
    r4 = NSTATE * nb
    a = lax.axis_index("atm")
    o = lax.axis_index("ocn")
    line = a * no + o

    nz = na // 4
    half = (a // 4) // (nz // 2)
    nx = no // 4

    def atm_peer(k):
        i = k // 4
        return (i * half + (nz - 1 - i) * (1 - half)) * 4 + k % 4

    def ocn_peer(k):
        rest = k % (no // 2)
        x = (o // 4 + rest // 2 + nx // 2) % nx
        z = (o // 2 + 1 + k // (no // 2)) % 2
        return x * 4 + z * 2 + (o + rest) % 2

    def each(count, peer, me, act):
        def step(k, carry):
            to = peer(k)

            @pl.when(to != me)
            def _():
                act(to)

            return carry

        lax.fori_loop(0, count, step, 0)

    barrier = pltpu.get_barrier_semaphore()

    def greet(device):
        pl.semaphore_signal(barrier, inc=1, device_id=device, device_id_type=MESH)

    each(no, ocn_peer, o, lambda to: greet((a, to)))
    each(na, atm_peer, a, lambda to: greet((to, o)))
    has_up, has_dn, has_left, has_right = a > 0, a < na - 1, o > 0, o < no - 1
    corners = []
    for dv, vert in ((-1, has_up), (1, has_dn)):
        @pl.when(vert)
        def _():
            greet((a + dv, no - 1 if dv < 0 else 0))

        for dh, hori in ((-1, has_left), (1, has_right)):
            corners.append((dv, dh, jnp.logical_and(vert, hori)))

            @pl.when(corners[-1][2])
            def _():
                greet((a + dv, o + dh))

    first = jnp.logical_and(o == 0, has_up)
    last = jnp.logical_and(o == no - 1, has_dn)
    greetings = na + no - 2 + no * (first.astype(jnp.int32) + last.astype(jnp.int32))
    for _, _, there in corners:
        greetings += there.astype(jnp.int32)

    copies = [
        pltpu.make_async_copy(src, dst, in_sem.at[i])
        for i, (src, dst) in enumerate((
            (cm_h, cm_v), (c_h, c_v), (atm_h, atm), (st_h, st), (mk_h, mk), (cm_h, cm_s), (pat_h, pat_s)))
    ]
    for copy in copies:
        copy.start()
    for d in range(no):
        pltpu.make_async_copy(w_h.at[d], w32.at[d], w_sem.at[d]).start()

    copies[0].wait()
    copies[1].wait()
    slot = iota((r4, na * nb), 1)
    cm = cm_v[...]
    mine = jnp.where(cm // nb == a, (cm % nb).astype(F32), 0.0)
    mine = jnp.where(slot // nb == iota((r4, na * nb), 0) // NSTATE, mine, 0.0)
    order = jnp.sum(mine, axis=1, keepdims=True).astype(jnp.int32)
    coeff = c_v[...]
    coeff = jnp.concatenate([coeff] * 2, axis=0)
    coeff = jnp.concatenate([coeff] * (C // F), axis=1)
    coeff = jnp.concatenate([coeff] * (r4 // 8), axis=0)
    coeff = jnp.concatenate([coeff] * (nb * F // C), axis=1)
    take = jnp.where(order == iota((r4, nb * F), 1) // F, coeff, 0.0)
    copies[2].wait()
    states = jnp.dot(take, atm[...], precision=HIGHEST, preferred_element_type=F32)
    for b in range(nb):
        out1[b] = states[NSTATE * b : NSTATE * b + NSTATE]
    arr1[a] = out1[a]

    copies[3].wait()
    copies[4].wait()
    land = mk[...].astype(F32)
    for b in range(no):
        mask_out[b] = land[2 * b : 2 * b + 2]
    mask_in[o] = mask_out[o]
    for s in range(NSTATE):
        a2_out[pl.ds(s, nb, stride=NSTATE), :] = land
    wet = a2_out[...]
    for s in range(NSTATE):
        a2_out[pl.ds(s, nb, stride=NSTATE), :] = st[s]
    tile = a2_out[...]
    turned, wet_turned = tile.T, wet.T
    for i in range(2):
        row_out[0, i] = tile[NSTATE * i : NSTATE * i + NSTATE]
        row_out[1, i] = tile[r4 - NSTATE * i - NSTATE : r4 - NSTATE * i]
        col_out[0, i : i + 1] = turned[i : i + 1]
        col_out[1, i : i + 1] = turned[C - 1 - i : C - i]
    row_out[0, 2] = wet[:NSTATE]
    row_out[1, 2] = wet[r4 - NSTATE :]
    col_out[0, 2:3] = wet_turned[:1]
    col_out[1, 2:3] = wet_turned[C - 1 :]
    for side in range(2):
        col_out[side, 3:4] = jnp.zeros((1, r4), F32)

    def row_copy(side, up_or_down, target):
        return pltpu.make_async_remote_copy(
            row_out.at[side], row_in.at[up_or_down], row_send.at[side], row_recv.at[up_or_down],
            device_id=(target, o), device_id_type=MESH)

    def col_copy(side, place, flight, target):
        return pltpu.make_async_remote_copy(
            col_out.at[side], col_in.at[place], col_send.at[flight], col_recv.at[place],
            device_id=target, device_id_type=MESH)

    halos = [
        (has_left, col_copy(0, 3, 2, (a, o - 1)), col_copy(0, 2, 2, (a, o - 1))),
        (has_right, col_copy(1, 2, 3, (a, o + 1)), col_copy(1, 3, 3, (a, o + 1))),
    ]
    for dv, dh, there in corners:
        side = 0 if dh < 0 else 1
        here = (0 if dv < 0 else 4) + side
        halos.append((there, col_copy(side, 5 - here, here, (a + dv, o + dh)), col_copy(side, here, here, (a + dv, o + dh))))
    halos.append((has_up, row_copy(0, 1, a - 1), row_copy(0, 0, a - 1)))
    halos.append((has_dn, row_copy(1, 0, a + 1), row_copy(1, 1, a + 1)))

    for side, inside in ((0, has_up), (1, has_dn)):
        @pl.when(jnp.logical_not(inside))
        def _():
            row_in[side] = jnp.zeros((3, NSTATE, C), F32)
            g_halo[side] = jnp.zeros((NSTATE, C), F32)

    places = [(2, has_left), (3, has_right)]
    places += [((0 if dv < 0 else 4) + (0 if dh < 0 else 1), there) for dv, dh, there in corners]
    for place, inside in places:
        @pl.when(jnp.logical_not(inside))
        def _():
            col_in[place] = jnp.zeros((4, r4), F32)

    has_above, has_below = line > 0, line < na * no - 1

    @pl.when(jnp.logical_not(has_above))
    def _():
        g_up[...] = jnp.zeros_like(g_up)

    @pl.when(jnp.logical_not(has_below))
    def _():
        g_dn[...] = jnp.zeros_like(g_dn)

    def block_copy(to):
        return pltpu.make_async_remote_copy(
            out1.at[to], arr1.at[a], x_send.at[0], x_recv.at[0], device_id=(to, o), device_id_type=MESH)

    def ocn_copy(i, src, dst, to):
        return pltpu.make_async_remote_copy(
            src, dst, x_send.at[i], x_recv.at[i], device_id=(a, to), device_id_type=MESH)

    def rows_of(d):
        return pl.ds(pl.multiple_of(8 * d, 8), 8)

    def alone(x):
        lane, state = iota((r4, C), 1), iota((r4, C), 0) % NSTATE
        none = jnp.zeros((NSTATE, C), F32)
        up = jnp.concatenate([none, x[: r4 - NSTATE]], axis=0)
        down = jnp.concatenate([x[NSTATE:], none], axis=0)
        left = jnp.where(lane == 0, 0.0, pltpu.roll(x, 1, 1))
        right = jnp.where(lane == C - 1, 0.0, pltpu.roll(x, C - 1, 1))
        return tend(x, up + down + left + right - 4.0 * x, wet, state)

    a2_part[...] = alone(alone(tile))
    pl.semaphore_wait(barrier, greetings)
    each(na, atm_peer, a, lambda to: block_copy(to).start())
    for there, copy, _ in halos:
        @pl.when(there)
        def _():
            copy.start()

    each(no, ocn_peer, o, lambda to: ocn_copy(1, mask_out.at[to], mask_in.at[o], to).start())

    copies[5].wait()
    copies[6].wait()
    for r in range(nb):
        idx_s[r] = cm_s[0, a * nb + pat_s[r]] // nb

    def split_weights(d, carry):
        pltpu.make_async_copy(w_h.at[d], w32.at[d], w_sem.at[d]).wait()
        w = w32[d]
        high = w.astype(BF16)
        whi[d] = high
        wlo[d] = (w - high.astype(F32)).astype(BF16)
        return carry

    lax.fori_loop(0, no, split_weights, 0)

    def a2_copy(src, to):
        return ocn_copy(2, src.at[rows_of(to)], a2_in.at[rows_of(o)], to)

    def send_inner(to):
        @pl.when(jnp.logical_and(to > 0, to < no - 1))
        def _():
            a2_copy(a2_part, to).start()

    each(no, ocn_peer, o, send_inner)

    for there, _, copy in halos:
        @pl.when(there)
        def _():
            copy.wait_recv()

    at, along_lane = iota((C, r4), 0), iota((C, r4), 1)
    beside = jnp.zeros((C, r4), F32)
    for i in range(3):
        beside = jnp.where(at == i, col_in[3, i : i + 1], beside)
        beside = jnp.where(at == C - 1 - i, col_in[2, i : i + 1], beside)
    diagonal = jnp.where(
        at == 0,
        jnp.where(along_lane < r4 // 2, col_in[5, :1], col_in[1, :1]),
        jnp.where(at == C - 1, jnp.where(along_lane < r4 // 2, col_in[4, :1], col_in[0, :1]), 0.0))
    beside, diagonal = beside.T, diagonal.T
    rows = r4 + 4 * NSTATE
    lane = iota((rows, C), 1)
    state = iota((rows, C), 0) % NSTATE
    none = jnp.zeros((NSTATE, C), F32)
    x = jnp.concatenate([row_in[0, 1], row_in[0, 0], tile, row_in[1, 0], row_in[1, 1]], axis=0)
    e = jnp.concatenate([none, diagonal[r4 - NSTATE :], beside, diagonal[:NSTATE], none], axis=0)
    wet_x = jnp.concatenate([none, row_in[0, 2], wet, row_in[1, 2], none], axis=0)
    wet_e = jnp.concatenate([none, none, beside, none, none], axis=0)
    wet_e = jnp.where(lane == 0, pltpu.roll(wet_e, C - 2, 1), jnp.where(lane == C - 1, pltpu.roll(wet_e, 2, 1), 0.0))

    def sides(x, e):
        x_right, e_right = pltpu.roll(x, 1, 1), pltpu.roll(e, 1, 1)
        x_left, e_left = pltpu.roll(x, C - 1, 1), pltpu.roll(e, C - 1, 1)
        low, high = iota(x.shape, 1) == 0, iota(x.shape, 1) == C - 1
        of_x = jnp.where(low, e_right, x_right) + jnp.where(high, e_left, x_left)
        of_e = jnp.where(low, x_right, e_right) + jnp.where(high, x_left, e_left)
        return of_x, of_e

    def rises(x):
        return pltpu.roll(x, NSTATE, 0) + pltpu.roll(x, rows - NSTATE, 0)

    of_x, of_e = sides(x, e)
    x, e = tend(x, rises(x) + of_x - 4.0 * x, wet_x, state), tend(e, rises(e) + of_e - 4.0 * e, wet_e, state)
    of_x, _ = sides(x, e)
    x = tend(x, rises(x) + of_x - 4.0 * x, wet_x, state)
    a2_out[...] = x[2 * NSTATE : 2 * NSTATE + r4]
    a2_in[rows_of(o)] = a2_out[rows_of(o)]
    for to in (0, no - 1):
        @pl.when(o != to)
        def _():
            a2_copy(a2_out, to).start()

    def by_pair(columns):
        lane, row = iota((r4, C), 1), iota((r4, C), 0) % 8
        found = jnp.zeros((r4, C), F32)
        for k, column in enumerate(columns):
            found = jnp.where(lane == row + 8 * k, column, found)
        return jnp.sum(found.reshape(no, 8, C), axis=1)

    def by_row(packed, k):
        lane, row = iota((r4, C), 1), iota((r4, C), 0) % 8
        return jnp.sum(jnp.where(lane == row + 8 * k, packed, 0.0), axis=1, keepdims=True)

    def spread(ref):
        return jnp.concatenate([jnp.broadcast_to(ref[d], (8, C)) for d in range(no)], axis=0)

    touched = (0, 1, C - 2, C - 1)
    added = a2_out[...] - a2_part[...]
    fix = by_pair([added[:, c : c + 1] for c in touched])
    for d in range(no):
        fix_out[d] = jnp.zeros((1, C), F32) if d in (0, no - 1) else fix[d : d + 1]
    fix_in[o] = jnp.zeros((1, C), F32)
    each(no, ocn_peer, o, lambda to: ocn_copy(5, fix_out.at[to], fix_in.at[o], to).start())

    def wait_all(i, ref, count, send):
        part = ref.at[pl.ds(0, count)]
        copy = ocn_copy(i, part, part, o)
        if send:
            copy.wait_send()
        else:
            copy.wait_recv()

    wait_all(1, mask_in, no - 1, False)
    wait_all(0, arr1, nb - 1, False)
    pairs = []
    for d in range(no):
        x = jnp.concatenate([arr1[idx_s[2 * d]], arr1[idx_s[2 * d + 1]]], axis=1)
        x = split(x)
        f = jnp.dot(x, whi[d], preferred_element_type=F32) + jnp.dot(x, wlo[d], preferred_element_type=F32)
        f = 0.25 * (f[:NSTATE] + f[NSTATE:])
        upper, lower = f[:, :C] * mask_in[d, 0:1], f[:, C:] * mask_in[d, 1:2]
        g[0, d] = upper
        g[1, d] = lower
        pairs.append(jnp.concatenate([upper, lower], axis=0))
        gx[8 * d : 8 * d + 8] = pairs[d]

    above = ((line - 1) // no, (line - 1) % no)
    below = ((line + 1) // no, (line + 1) % no)

    def g_copy(row, dst, place, target):
        return pltpu.make_async_remote_copy(
            g.at[row], dst, g_send.at[row], g_recv.at[place], device_id=target, device_id_type=MESH)

    def halo_copy(row, d, target):
        return pltpu.make_async_remote_copy(
            g.at[row, d], g_halo.at[1 - row], h_send.at[row], h_recv.at[1 - row],
            device_id=(target, d), device_id_type=MESH)

    @pl.when(has_above)
    def _():
        g_copy(0, g_dn, 1, above).start()

    @pl.when(has_below)
    def _():
        g_copy(1, g_up, 0, below).start()

    @pl.when(first)
    def _():
        for d in range(no):
            halo_copy(0, d, a - 1).start()

    @pl.when(last)
    def _():
        for d in range(no):
            halo_copy(1, d, a + 1).start()

    each(no, ocn_peer, o, lambda to: ocn_copy(3, gx.at[rows_of(to)], g_in.at[rows_of(o)], to).start())
    g_in[rows_of(o)] = gx[rows_of(o)]

    whole = gx[...]
    one = jnp.zeros((8, 1), F32)
    edge = by_pair([
        jnp.concatenate([one, whole[: r4 - 8, C - 1 :]], axis=0),
        jnp.concatenate([whole[8:, :1], one], axis=0)])
    for d in range(no):
        edge_out[d] = edge[d : d + 1]
    each(no, ocn_peer, o, lambda to: ocn_copy(4, edge_out.at[to], edge_in.at[o], to).start())
    edge_in[o] = edge_out[o]
    lane8, row8 = iota((8, C), 1), iota((8, C), 0)
    nothing = jnp.zeros((8, C), F32)
    lefts = [pltpu.roll(x, 1, 1) for x in pairs]
    rights = [pltpu.roll(x, C - 1, 1) for x in pairs]

    wait_all(2, a2_in, 8 * (no - 1), False)
    wait_all(5, fix_in, no - 1, False)
    packed = spread(fix_in)
    x = a2_in[...]
    for k, c in enumerate(touched):
        x = x + jnp.where(iota((r4, C), 1) == c, by_row(packed, k), 0.0)
    a2_in[...] = x

    @pl.when(has_above)
    def _():
        g_copy(0, g_up, 0, above).wait_recv()

    @pl.when(has_below)
    def _():
        g_copy(1, g_dn, 1, below).wait_recv()

    nt = (((1,), (1,)), ((), ()))
    for d in range(no):
        x = pairs[d]
        up = jnp.concatenate([g_up[d], x[:NSTATE]], axis=0)
        down = jnp.concatenate([x[NSTATE:], g_dn[d]], axis=0)
        left = jnp.where(lane8 == 0, lefts[d - 1] if d > 0 else nothing, lefts[d])
        right = jnp.where(lane8 == C - 1, rights[d + 1] if d < no - 1 else nothing, rights[d])
        wet8 = jnp.where(row8 < NSTATE, mask_in[d, 0:1], mask_in[d, 1:2])
        x = a2_in[8 * d : 8 * d + 8] + (x + tend(x, up + down + left + right - 4.0 * x, wet8, row8 % NSTATE))
        x = split(jnp.concatenate([x[:NSTATE], x[NSTATE:]], axis=1))
        f = lax.dot_general(x, whi[d], nt, preferred_element_type=F32) + lax.dot_general(
            x, wlo[d], nt, preferred_element_type=F32)
        f = f[:NSTATE] + f[NSTATE:]
        back[8 * d : 8 * d + 8] = jnp.concatenate([f[:, :C], f[:, C:]], axis=0)

    wait_all(3, g_in, 8 * (no - 1), False)
    wait_all(4, edge_in, no - 1, False)

    @pl.when(has_up)
    def _():
        halo_copy(1, 0, a).wait_recv()

    @pl.when(has_dn)
    def _():
        halo_copy(0, 0, a).wait_recv()

    x = g_in[...]
    edge = spread(edge_in)
    lane, row = iota((r4, C), 1), iota((r4, C), 0)
    before, after = by_row(edge, 0), by_row(edge, 1)
    up = jnp.concatenate([g_halo[0], x[: r4 - NSTATE]], axis=0)
    down = jnp.concatenate([x[NSTATE:], g_halo[1]], axis=0)
    left = jnp.where(lane == 0, before, pltpu.roll(x, 1, 1))
    right = jnp.where(lane == C - 1, after, pltpu.roll(x, C - 1, 1))
    flat[...] = a2_out[...] + (x + tend(x, up + down + left + right - 4.0 * x, wet, row % NSTATE))

    wait_all(0, out1, nb - 1, True)
    wait_all(1, mask_out, no - 1, True)
    wait_all(2, a2_out, 8 * (no - 1), True)
    wait_all(3, gx, 8 * (no - 1), True)
    wait_all(4, edge_out, no - 1, True)
    wait_all(5, fix_out, no - 1, True)
    for there, copy, _ in halos:
        @pl.when(there)
        def _():
            copy.wait_send()

    @pl.when(has_above)
    def _():
        g_copy(0, g_dn, 1, above).wait_send()

    @pl.when(has_below)
    def _():
        g_copy(1, g_up, 0, below).wait_send()

    for row, sends in ((0, first), (1, last)):
        @pl.when(sends)
        def _():
            pltpu.make_async_remote_copy(
                g.at[row], g_up, h_send.at[row], h_recv.at[1 - row], device_id=(a, o), device_id_type=MESH).wait_send()


def finish(nb, pat_s, flat, back, on, returned):
    for s in range(NSTATE):
        on[s] = flat[pl.ds(s, nb, stride=NSTATE), :]
    for r in range(nb):
        returned[pat_s[r]] = back[NSTATE * r : NSTATE * r + NSTATE]


def body(na, no, atm_fields, coupler_map, remap_pattern, remap_weights, bulk_coeffs, ocean_state, land_mask):
    nb = atm_fields.shape[0]
    r4 = NSTATE * nb
    any_space = pl.BlockSpec(memory_space=pl.ANY)
    vmem = pl.BlockSpec(memory_space=pltpu.VMEM)
    dma = pltpu.SemaphoreType.DMA
    flat, back = pl.pallas_call(
        functools.partial(kernel, na, no),
        out_shape=(pltpu.VMEM((r4, C), F32), pltpu.VMEM((r4, C), F32)),
        in_specs=[any_space] * 7,
        out_specs=(vmem, vmem),
        scratch_shapes=[
            pltpu.VMEM((1, na * nb), jnp.int32),
            pltpu.SMEM((1, na * nb), jnp.int32),
            pltpu.SMEM((nb,), jnp.int32),
            pltpu.VMEM((NSTATE, F), F32),
            pltpu.VMEM((nb * F, C), F32),
            pltpu.VMEM((no, 2 * C, 2 * C), F32),
            pltpu.VMEM((no, 2 * C, 2 * C), BF16),
            pltpu.VMEM((no, 2 * C, 2 * C), BF16),
            pltpu.VMEM((NSTATE, nb, C), F32),
            pltpu.VMEM((nb, C), jnp.int32),
            pltpu.VMEM((nb, NSTATE, C), F32),
            pltpu.VMEM((nb, NSTATE, C), F32),
            pltpu.SMEM((nb,), jnp.int32),
            pltpu.VMEM((2, 3, NSTATE, C), F32),
            pltpu.VMEM((2, 3, NSTATE, C), F32),
            pltpu.VMEM((2, 4, r4), F32),
            pltpu.VMEM((6, 4, r4), F32),
            pltpu.VMEM((no, 2, C), F32),
            pltpu.VMEM((no, 2, C), F32),
            pltpu.VMEM((r4, C), F32),
            pltpu.VMEM((r4, C), F32),
            pltpu.VMEM((r4, C), F32),
            pltpu.VMEM((no, 1, C), F32),
            pltpu.VMEM((no, 1, C), F32),
            pltpu.VMEM((2, no, NSTATE, C), F32),
            pltpu.VMEM((no, NSTATE, C), F32),
            pltpu.VMEM((no, NSTATE, C), F32),
            pltpu.VMEM((r4, C), F32),
            pltpu.VMEM((r4, C), F32),
            pltpu.VMEM((no, 1, C), F32),
            pltpu.VMEM((no, 1, C), F32),
            pltpu.VMEM((2, NSTATE, C), F32),
            dma((7,)),
            dma((no,)),
            dma((6,)),
            dma((6,)),
            dma((2,)),
            dma((2,)),
            dma((6,)),
            dma((6,)),
            dma((2,)),
            dma((2,)),
            dma((2,)),
            dma((2,)),
        ],
        compiler_params=pltpu.CompilerParams(
            collective_id=0, has_side_effects=True, vmem_limit_bytes=60 * 1024 * 1024
        ),
    )(
        atm_fields.reshape(nb * F, C),
        remap_weights.reshape(no, 2 * C, 2 * C),
        ocean_state,
        land_mask,
        coupler_map,
        remap_pattern,
        bulk_coeffs,
    )
    return pl.pallas_call(
        functools.partial(finish, nb),
        out_shape=(
            jax.ShapeDtypeStruct(ocean_state.shape, F32),
            jax.ShapeDtypeStruct((nb, NSTATE, C), F32),
        ),
        in_specs=[pl.BlockSpec(memory_space=pltpu.SMEM), vmem, vmem],
        out_specs=(vmem, vmem),
        compiler_params=pltpu.CompilerParams(vmem_limit_bytes=4 * 1024 * 1024),
    )(remap_pattern, flat, back)


def solution(mesh):
    in_specs = (
        P(("atm", "ocn"), None, None),
        P("ocn", None),
        P(("atm", "ocn")),
        P(("atm", "ocn"), None, None),
        P(),
        P(None, "atm", "ocn"),
        P("atm", "ocn"),
    )
    out_specs = (P(None, "atm", "ocn"), P(("atm", "ocn"), None, None))
    step = functools.partial(body, mesh.shape["atm"], mesh.shape["ocn"])
    return jax.shard_map(step, mesh=mesh, in_specs=in_specs, out_specs=out_specs, check_vma=False)
```

```python
import functools

import jax
import jax.numpy as jnp
from jax import lax
from jax.experimental import pallas as pl
from jax.experimental.pallas import tpu as pltpu
from jax.sharding import PartitionSpec as P

MESH = pl.DeviceIdType.MESH
F32 = jnp.float32
BF16 = jnp.bfloat16
NSTATE = 4
F = 16
C = 128
HIGHEST = lax.Precision.HIGHEST


def iota(shape, dim):
    return lax.broadcasted_iota(jnp.int32, shape, dim)


def split(x):
    high = x.astype(BF16).astype(F32)
    return jnp.concatenate([high, x - high], axis=0).astype(BF16)


def tend(x, lap, mask, state):
    rows = x.shape[0]
    rot = jnp.where(
        state == 0,
        pltpu.roll(x, rows - 1, 0),
        jnp.where(state == 1, -pltpu.roll(x, 1, 0), 0.0),
    )
    kappa = jnp.where(state < 2, F32(0.8), F32(0.5))
    return mask * (x + 0.25 * (kappa * lap + 0.5 * rot - 0.1 * x))


def kernel(
    na, no,
    atm_h, w_h, st_h, mk_h, cm_h, pat_h, c_h,
    on, returned,
    cm_v, cm_s, pat_s, c_v,
    atm, w32, whi, wlo, st, mk,
    out1, arr1, idx_s,
    row_out, row_in, col_out, col_in,
    mask_out, mask_in, a2_out, a2_in, a2_part, fix_out, fix_in,
    g, g_up, g_dn, gx, g_in, edge_out, edge_in, g_halo, back,
    in_sem, w_sem, x_send, x_recv, row_send, row_recv, col_send, col_recv, g_send, g_recv, h_send, h_recv,
):
    nb = na
    r4 = NSTATE * nb
    a = lax.axis_index("atm")
    o = lax.axis_index("ocn")
    line = a * no + o

    nz, nx = na // 4, no // 4
    zs = [lax.rem(lax.div(a, 4) + k, nz) * 4 for k in range(nz)]
    ys = [lax.rem(lax.rem(a, 4) + k, 4) for k in range(4)]
    xs = [lax.rem(lax.div(o, 4) + k, nx) * 4 for k in range(nx)]
    hs = [lax.rem(lax.div(o, 2) + k, 2) * 2 for k in range(2)]
    cs = [lax.rem(o + k, 2) for k in range(2)]
    z_order = [k for i in range(1, nz // 2 + 1) for k in ((nz - i, i) if nz - i != i else (i,))]
    atm_far = [zs[k] + ys[y] for k in z_order for y in (2, 1, 3, 0)]
    atm_near = [zs[0] + ys[y] for y in (2, 1, 3)]
    x_order = [nx // 2] + [k for k in range(nx) if k != nx // 2]
    ocn_far = [xs[k] + hs[1] + cs[c] for k in x_order for c in (1, 0)]
    ocn_near = [xs[k] + hs[0] + cs[c] for k in x_order for c in (1, 0) if k or c]
    atm_peers, ocn_peers = atm_far + atm_near, ocn_far + ocn_near

    barrier = pltpu.get_barrier_semaphore()

    def greet(device):
        pl.semaphore_signal(barrier, inc=1, device_id=device, device_id_type=MESH)

    for to in ocn_far:
        greet((a, to))
    for to in atm_far:
        greet((to, o))
    has_up, has_dn, has_left, has_right = a > 0, a < na - 1, o > 0, o < no - 1
    corners = []
    for dv, vert in ((-1, has_up), (1, has_dn)):
        @pl.when(vert)
        def _():
            greet((a + dv, no - 1 if dv < 0 else 0))

        for dh, hori in ((-1, has_left), (1, has_right)):
            corners.append((dv, dh, jnp.logical_and(vert, hori)))

            @pl.when(corners[-1][2])
            def _():
                greet((a + dv, o + dh))

    for to in ocn_near:
        greet((a, to))
    for to in atm_near:
        greet((to, o))
    first = jnp.logical_and(o == 0, has_up)
    last = jnp.logical_and(o == no - 1, has_dn)
    greetings = na + no - 2 + no * (first.astype(jnp.int32) + last.astype(jnp.int32))
    for _, _, there in corners:
        greetings += there.astype(jnp.int32)

    copies = [
        pltpu.make_async_copy(src, dst, in_sem.at[i])
        for i, (src, dst) in enumerate((
            (cm_h, cm_v), (c_h, c_v), (atm_h, atm), (st_h, st), (mk_h, mk), (cm_h, cm_s), (pat_h, pat_s)))
    ]
    for copy in copies:
        copy.start()
    for d in range(no):
        pltpu.make_async_copy(w_h.at[d], w32.at[d], w_sem.at[d]).start()

    copies[0].wait()
    copies[1].wait()
    slot = iota((r4, na * nb), 1)
    cm = cm_v[...]
    mine = jnp.where(cm // nb == a, (cm % nb).astype(F32), 0.0)
    mine = jnp.where(slot // nb == iota((r4, na * nb), 0) // NSTATE, mine, 0.0)
    order = jnp.sum(mine, axis=1, keepdims=True).astype(jnp.int32)
    coeff = c_v[...]
    coeff = jnp.concatenate([coeff] * 2, axis=0)
    coeff = jnp.concatenate([coeff] * (C // F), axis=1)
    coeff = jnp.concatenate([coeff] * (r4 // 8), axis=0)
    coeff = jnp.concatenate([coeff] * (nb * F // C), axis=1)
    take = jnp.where(order == iota((r4, nb * F), 1) // F, coeff, 0.0)
    copies[2].wait()
    states = jnp.dot(take, atm[...], precision=HIGHEST, preferred_element_type=F32)
    for b in range(nb):
        out1[b] = states[NSTATE * b : NSTATE * b + NSTATE]
    arr1[a] = out1[a]

    copies[3].wait()
    copies[4].wait()
    land = mk[...].astype(F32)
    for b in range(no):
        mask_out[b] = land[2 * b : 2 * b + 2]
    mask_in[o] = mask_out[o]
    for s in range(NSTATE):
        a2_out[pl.ds(s, nb, stride=NSTATE), :] = land
    wet = a2_out[...]
    for s in range(NSTATE):
        a2_out[pl.ds(s, nb, stride=NSTATE), :] = st[s]
    tile = a2_out[...]
    turned, wet_turned = tile.T, wet.T
    for i in range(2):
        row_out[0, i] = tile[NSTATE * i : NSTATE * i + NSTATE]
        row_out[1, i] = tile[r4 - NSTATE * i - NSTATE : r4 - NSTATE * i]
        col_out[0, i : i + 1] = turned[i : i + 1]
        col_out[1, i : i + 1] = turned[C - 1 - i : C - i]
    row_out[0, 2] = wet[:NSTATE]
    row_out[1, 2] = wet[r4 - NSTATE :]
    col_out[0, 2:3] = wet_turned[:1]
    col_out[1, 2:3] = wet_turned[C - 1 :]
    for side in range(2):
        col_out[side, 3:4] = jnp.zeros((1, r4), F32)

    def row_copy(side, up_or_down, target):
        return pltpu.make_async_remote_copy(
            row_out.at[side], row_in.at[up_or_down], row_send.at[side], row_recv.at[up_or_down],
            device_id=(target, o), device_id_type=MESH)

    def col_copy(side, place, flight, target):
        return pltpu.make_async_remote_copy(
            col_out.at[side], col_in.at[place], col_send.at[flight], col_recv.at[place],
            device_id=target, device_id_type=MESH)

    halos = [
        (has_left, col_copy(0, 3, 2, (a, o - 1)), col_copy(0, 2, 2, (a, o - 1))),
        (has_right, col_copy(1, 2, 3, (a, o + 1)), col_copy(1, 3, 3, (a, o + 1))),
    ]
    for dv, dh, there in corners:
        side = 0 if dh < 0 else 1
        here = (0 if dv < 0 else 4) + side
        halos.append((there, col_copy(side, 5 - here, here, (a + dv, o + dh)), col_copy(side, here, here, (a + dv, o + dh))))
    halos.append((has_up, row_copy(0, 1, a - 1), row_copy(0, 0, a - 1)))
    halos.append((has_dn, row_copy(1, 0, a + 1), row_copy(1, 1, a + 1)))

    for side, inside in ((0, has_up), (1, has_dn)):
        @pl.when(jnp.logical_not(inside))
        def _():
            row_in[side] = jnp.zeros((3, NSTATE, C), F32)
            g_halo[side] = jnp.zeros((NSTATE, C), F32)

    places = [(2, has_left), (3, has_right)]
    places += [((0 if dv < 0 else 4) + (0 if dh < 0 else 1), there) for dv, dh, there in corners]
    for place, inside in places:
        @pl.when(jnp.logical_not(inside))
        def _():
            col_in[place] = jnp.zeros((4, r4), F32)

    has_above, has_below = line > 0, line < na * no - 1

    @pl.when(jnp.logical_not(has_above))
    def _():
        g_up[...] = jnp.zeros_like(g_up)

    @pl.when(jnp.logical_not(has_below))
    def _():
        g_dn[...] = jnp.zeros_like(g_dn)

    def block_copy(to):
        return pltpu.make_async_remote_copy(
            out1.at[to], arr1.at[a], x_send.at[0], x_recv.at[0], device_id=(to, o), device_id_type=MESH)

    def ocn_copy(i, src, dst, to):
        return pltpu.make_async_remote_copy(
            src, dst, x_send.at[i], x_recv.at[i], device_id=(a, to), device_id_type=MESH)

    def rows_of(d):
        return pl.ds(pl.multiple_of(8 * d, 8), 8)

    def alone(x):
        lane, state = iota((r4, C), 1), iota((r4, C), 0) % NSTATE
        none = jnp.zeros((NSTATE, C), F32)
        up = jnp.concatenate([none, x[: r4 - NSTATE]], axis=0)
        down = jnp.concatenate([x[NSTATE:], none], axis=0)
        left = jnp.where(lane == 0, 0.0, pltpu.roll(x, 1, 1))
        right = jnp.where(lane == C - 1, 0.0, pltpu.roll(x, C - 1, 1))
        return tend(x, up + down + left + right - 4.0 * x, wet, state)

    a2_part[...] = alone(alone(tile))
    pl.semaphore_wait(barrier, greetings)
    for to in atm_far[: na // 2]:
        block_copy(to).start()
    for to in ocn_far:
        ocn_copy(1, mask_out.at[to], mask_in.at[o], to).start()
    for to in atm_far[na // 2 :] + atm_near:
        block_copy(to).start()
    for to in ocn_near:
        ocn_copy(1, mask_out.at[to], mask_in.at[o], to).start()
    for there, copy, _ in halos:
        @pl.when(there)
        def _():
            copy.start()

    copies[5].wait()
    copies[6].wait()
    for r in range(nb):
        idx_s[r] = cm_s[0, a * nb + pat_s[r]] // nb

    def split_weights(d, carry):
        pltpu.make_async_copy(w_h.at[d], w32.at[d], w_sem.at[d]).wait()
        w = w32[d]
        high = w.astype(BF16)
        whi[d] = high
        wlo[d] = (w - high.astype(F32)).astype(BF16)
        return carry

    lax.fori_loop(0, no, split_weights, 0)

    across = iota((r4, r4), 1)
    along = iota((r4, r4), 0)
    pattern = jnp.zeros((1, r4), jnp.int32)
    for r in range(nb):
        pattern = jnp.where(iota((1, r4), 1) // NSTATE == r, pat_s[r], pattern)
    place = jnp.logical_and(pattern == along // NSTATE, across % NSTATE == along % NSTATE)
    place = jnp.where(place, 1.0, 0.0).astype(F32)

    def a2_copy(src, to):
        return ocn_copy(2, src.at[rows_of(to)], a2_in.at[rows_of(o)], to)

    def send_inner(to):
        @pl.when(jnp.logical_and(to > 0, to < no - 1))
        def _():
            a2_copy(a2_part, to).start()

    for to in ocn_peers:
        send_inner(to)

    for there, _, copy in halos:
        @pl.when(there)
        def _():
            copy.wait_recv()

    at, along_lane = iota((C, r4), 0), iota((C, r4), 1)
    beside = jnp.zeros((C, r4), F32)
    for i in range(3):
        beside = jnp.where(at == i, col_in[3, i : i + 1], beside)
        beside = jnp.where(at == C - 1 - i, col_in[2, i : i + 1], beside)
    diagonal = jnp.where(
        at == 0,
        jnp.where(along_lane < r4 // 2, col_in[5, :1], col_in[1, :1]),
        jnp.where(at == C - 1, jnp.where(along_lane < r4 // 2, col_in[4, :1], col_in[0, :1]), 0.0))
    beside, diagonal = beside.T, diagonal.T
    rows = r4 + 4 * NSTATE
    lane = iota((rows, C), 1)
    state = iota((rows, C), 0) % NSTATE
    none = jnp.zeros((NSTATE, C), F32)
    x = jnp.concatenate([row_in[0, 1], row_in[0, 0], tile, row_in[1, 0], row_in[1, 1]], axis=0)
    e = jnp.concatenate([none, diagonal[r4 - NSTATE :], beside, diagonal[:NSTATE], none], axis=0)
    wet_x = jnp.concatenate([none, row_in[0, 2], wet, row_in[1, 2], none], axis=0)
    wet_e = jnp.concatenate([none, none, beside, none, none], axis=0)
    wet_e = jnp.where(lane == 0, pltpu.roll(wet_e, C - 2, 1), jnp.where(lane == C - 1, pltpu.roll(wet_e, 2, 1), 0.0))

    def sides(x, e):
        x_right, e_right = pltpu.roll(x, 1, 1), pltpu.roll(e, 1, 1)
        x_left, e_left = pltpu.roll(x, C - 1, 1), pltpu.roll(e, C - 1, 1)
        low, high = iota(x.shape, 1) == 0, iota(x.shape, 1) == C - 1
        of_x = jnp.where(low, e_right, x_right) + jnp.where(high, e_left, x_left)
        of_e = jnp.where(low, x_right, e_right) + jnp.where(high, x_left, e_left)
        return of_x, of_e

    def rises(x):
        return pltpu.roll(x, NSTATE, 0) + pltpu.roll(x, rows - NSTATE, 0)

    of_x, of_e = sides(x, e)
    x, e = tend(x, rises(x) + of_x - 4.0 * x, wet_x, state), tend(e, rises(e) + of_e - 4.0 * e, wet_e, state)
    of_x, _ = sides(x, e)
    x = tend(x, rises(x) + of_x - 4.0 * x, wet_x, state)
    a2_out[...] = x[2 * NSTATE : 2 * NSTATE + r4]
    a2_in[rows_of(o)] = a2_out[rows_of(o)]
    for to in (0, no - 1):
        @pl.when(o != to)
        def _():
            a2_copy(a2_out, to).start()

    def by_pair(columns):
        lane, row = iota((r4, C), 1), iota((r4, C), 0) % 8
        found = jnp.zeros((r4, C), F32)
        for k, column in enumerate(columns):
            found = jnp.where(lane == row + 8 * k, column, found)
        return jnp.sum(found.reshape(no, 8, C), axis=1)

    def by_row(packed, k):
        lane, row = iota((r4, C), 1), iota((r4, C), 0) % 8
        return jnp.sum(jnp.where(lane == row + 8 * k, packed, 0.0), axis=1, keepdims=True)

    def spread(ref):
        return jnp.concatenate([jnp.broadcast_to(ref[d], (8, C)) for d in range(no)], axis=0)

    touched = (0, 1, C - 2, C - 1)
    added = a2_out[...] - a2_part[...]
    fix = by_pair([added[:, c : c + 1] for c in touched])
    for d in range(no):
        fix_out[d] = jnp.zeros((1, C), F32) if d in (0, no - 1) else fix[d : d + 1]
    fix_in[o] = jnp.zeros((1, C), F32)
    for to in ocn_peers:
        ocn_copy(5, fix_out.at[to], fix_in.at[o], to).start()

    def wait_all(i, ref, count, send):
        part = ref.at[pl.ds(0, count)]
        copy = ocn_copy(i, part, part, o)
        if send:
            copy.wait_send()
        else:
            copy.wait_recv()

    wait_all(1, mask_in, no - 1, False)
    wait_all(0, arr1, nb - 1, False)
    pairs = []
    for d in range(no):
        x = jnp.concatenate([arr1[idx_s[2 * d]], arr1[idx_s[2 * d + 1]]], axis=1)
        x = split(x)
        f = jnp.dot(x, whi[d], preferred_element_type=F32) + jnp.dot(x, wlo[d], preferred_element_type=F32)
        f = 0.25 * (f[:NSTATE] + f[NSTATE:])
        upper, lower = f[:, :C] * mask_in[d, 0:1], f[:, C:] * mask_in[d, 1:2]
        g[0, d] = upper
        g[1, d] = lower
        pairs.append(jnp.concatenate([upper, lower], axis=0))
        gx[8 * d : 8 * d + 8] = pairs[d]

    above = ((line - 1) // no, (line - 1) % no)
    below = ((line + 1) // no, (line + 1) % no)

    def g_copy(row, dst, place, target):
        return pltpu.make_async_remote_copy(
            g.at[row], dst, g_send.at[row], g_recv.at[place], device_id=target, device_id_type=MESH)

    def halo_copy(row, d, target):
        return pltpu.make_async_remote_copy(
            g.at[row, d], g_halo.at[1 - row], h_send.at[row], h_recv.at[1 - row],
            device_id=(target, d), device_id_type=MESH)

    @pl.when(has_above)
    def _():
        g_copy(0, g_dn, 1, above).start()

    @pl.when(has_below)
    def _():
        g_copy(1, g_up, 0, below).start()

    @pl.when(first)
    def _():
        for d in range(no):
            halo_copy(0, d, a - 1).start()

    @pl.when(last)
    def _():
        for d in range(no):
            halo_copy(1, d, a + 1).start()

    for to in ocn_peers:
        ocn_copy(3, gx.at[rows_of(to)], g_in.at[rows_of(o)], to).start()
    g_in[rows_of(o)] = gx[rows_of(o)]

    whole = gx[...]
    one = jnp.zeros((8, 1), F32)
    edge = by_pair([
        jnp.concatenate([one, whole[: r4 - 8, C - 1 :]], axis=0),
        jnp.concatenate([whole[8:, :1], one], axis=0)])
    for d in range(no):
        edge_out[d] = edge[d : d + 1]
    for to in ocn_peers:
        ocn_copy(4, edge_out.at[to], edge_in.at[o], to).start()
    edge_in[o] = edge_out[o]
    lane8, row8 = iota((8, C), 1), iota((8, C), 0)
    nothing = jnp.zeros((8, C), F32)
    lefts = [pltpu.roll(x, 1, 1) for x in pairs]
    rights = [pltpu.roll(x, C - 1, 1) for x in pairs]

    wait_all(2, a2_in, 8 * (no - 1), False)
    wait_all(5, fix_in, no - 1, False)
    packed = spread(fix_in)
    x = a2_in[...]
    for k, c in enumerate(touched):
        x = x + jnp.where(iota((r4, C), 1) == c, by_row(packed, k), 0.0)
    a2_in[...] = x

    @pl.when(has_above)
    def _():
        g_copy(0, g_up, 0, above).wait_recv()

    @pl.when(has_below)
    def _():
        g_copy(1, g_dn, 1, below).wait_recv()

    nt = (((1,), (1,)), ((), ()))
    for d in range(no):
        x = pairs[d]
        up = jnp.concatenate([g_up[d], x[:NSTATE]], axis=0)
        down = jnp.concatenate([x[NSTATE:], g_dn[d]], axis=0)
        left = jnp.where(lane8 == 0, lefts[d - 1] if d > 0 else nothing, lefts[d])
        right = jnp.where(lane8 == C - 1, rights[d + 1] if d < no - 1 else nothing, rights[d])
        wet8 = jnp.where(row8 < NSTATE, mask_in[d, 0:1], mask_in[d, 1:2])
        x = a2_in[8 * d : 8 * d + 8] + (x + tend(x, up + down + left + right - 4.0 * x, wet8, row8 % NSTATE))
        x = split(jnp.concatenate([x[:NSTATE], x[NSTATE:]], axis=1))
        f = lax.dot_general(x, whi[d], nt, preferred_element_type=F32) + lax.dot_general(
            x, wlo[d], nt, preferred_element_type=F32)
        f = f[:NSTATE] + f[NSTATE:]
        back[8 * d : 8 * d + 8] = jnp.concatenate([f[:, :C], f[:, C:]], axis=0)

    placed = jnp.dot(place, back[...], precision=HIGHEST, preferred_element_type=F32)
    for b in range(nb):
        returned[b] = placed[NSTATE * b : NSTATE * b + NSTATE]

    wait_all(3, g_in, 8 * (no - 1), False)
    wait_all(4, edge_in, no - 1, False)

    @pl.when(has_up)
    def _():
        halo_copy(1, 0, a).wait_recv()

    @pl.when(has_dn)
    def _():
        halo_copy(0, 0, a).wait_recv()

    x = g_in[...]
    edge = spread(edge_in)
    lane, row = iota((r4, C), 1), iota((r4, C), 0)
    before, after = by_row(edge, 0), by_row(edge, 1)
    up = jnp.concatenate([g_halo[0], x[: r4 - NSTATE]], axis=0)
    down = jnp.concatenate([x[NSTATE:], g_halo[1]], axis=0)
    left = jnp.where(lane == 0, before, pltpu.roll(x, 1, 1))
    right = jnp.where(lane == C - 1, after, pltpu.roll(x, C - 1, 1))
    back[...] = a2_out[...] + (x + tend(x, up + down + left + right - 4.0 * x, wet, row % NSTATE))
    for s in range(NSTATE):
        on[s] = back[pl.ds(s, nb, stride=NSTATE), :]

    wait_all(0, out1, nb - 1, True)
    wait_all(1, mask_out, no - 1, True)
    wait_all(2, a2_out, 8 * (no - 1), True)
    wait_all(3, gx, 8 * (no - 1), True)
    wait_all(4, edge_out, no - 1, True)
    wait_all(5, fix_out, no - 1, True)
    for there, copy, _ in halos:
        @pl.when(there)
        def _():
            copy.wait_send()

    @pl.when(has_above)
    def _():
        g_copy(0, g_dn, 1, above).wait_send()

    @pl.when(has_below)
    def _():
        g_copy(1, g_up, 0, below).wait_send()

    for row, sends in ((0, first), (1, last)):
        @pl.when(sends)
        def _():
            pltpu.make_async_remote_copy(
                g.at[row], g_up, h_send.at[row], h_recv.at[1 - row], device_id=(a, o), device_id_type=MESH).wait_send()


def finish(on, returned, on_h, returned_h, sems):
    copies = [pltpu.make_async_copy(on, on_h, sems.at[0]), pltpu.make_async_copy(returned, returned_h, sems.at[1])]
    for copy in copies:
        copy.start()
    for copy in copies:
        copy.wait()


def body(na, no, atm_fields, coupler_map, remap_pattern, remap_weights, bulk_coeffs, ocean_state, land_mask):
    nb = atm_fields.shape[0]
    r4 = NSTATE * nb
    any_space = pl.BlockSpec(memory_space=pl.ANY)
    vmem = pl.BlockSpec(memory_space=pltpu.VMEM)
    dma = pltpu.SemaphoreType.DMA
    on, returned = pl.pallas_call(
        functools.partial(kernel, na, no),
        out_shape=(pltpu.VMEM((NSTATE, nb, C), F32), pltpu.VMEM((nb, NSTATE, C), F32)),
        in_specs=[any_space] * 7,
        out_specs=(vmem, vmem),
        scratch_shapes=[
            pltpu.VMEM((1, na * nb), jnp.int32),
            pltpu.SMEM((1, na * nb), jnp.int32),
            pltpu.SMEM((nb,), jnp.int32),
            pltpu.VMEM((NSTATE, F), F32),
            pltpu.VMEM((nb * F, C), F32),
            pltpu.VMEM((no, 2 * C, 2 * C), F32),
            pltpu.VMEM((no, 2 * C, 2 * C), BF16),
            pltpu.VMEM((no, 2 * C, 2 * C), BF16),
            pltpu.VMEM((NSTATE, nb, C), F32),
            pltpu.VMEM((nb, C), jnp.int32),
            pltpu.VMEM((nb, NSTATE, C), F32),
            pltpu.VMEM((nb, NSTATE, C), F32),
            pltpu.SMEM((nb,), jnp.int32),
            pltpu.VMEM((2, 3, NSTATE, C), F32),
            pltpu.VMEM((2, 3, NSTATE, C), F32),
            pltpu.VMEM((2, 4, r4), F32),
            pltpu.VMEM((6, 4, r4), F32),
            pltpu.VMEM((no, 2, C), F32),
            pltpu.VMEM((no, 2, C), F32),
            pltpu.VMEM((r4, C), F32),
            pltpu.VMEM((r4, C), F32),
            pltpu.VMEM((r4, C), F32),
            pltpu.VMEM((no, 1, C), F32),
            pltpu.VMEM((no, 1, C), F32),
            pltpu.VMEM((2, no, NSTATE, C), F32),
            pltpu.VMEM((no, NSTATE, C), F32),
            pltpu.VMEM((no, NSTATE, C), F32),
            pltpu.VMEM((r4, C), F32),
            pltpu.VMEM((r4, C), F32),
            pltpu.VMEM((no, 1, C), F32),
            pltpu.VMEM((no, 1, C), F32),
            pltpu.VMEM((2, NSTATE, C), F32),
            pltpu.VMEM((r4, C), F32),
            dma((7,)),
            dma((no,)),
            dma((6,)),
            dma((6,)),
            dma((2,)),
            dma((2,)),
            dma((6,)),
            dma((6,)),
            dma((2,)),
            dma((2,)),
            dma((2,)),
            dma((2,)),
        ],
        compiler_params=pltpu.CompilerParams(
            collective_id=0, has_side_effects=True, vmem_limit_bytes=60 * 1024 * 1024
        ),
    )(
        atm_fields.reshape(nb * F, C),
        remap_weights.reshape(no, 2 * C, 2 * C),
        ocean_state,
        land_mask,
        coupler_map,
        remap_pattern,
        bulk_coeffs,
    )
    return pl.pallas_call(
        finish,
        out_shape=(
            jax.ShapeDtypeStruct(ocean_state.shape, F32),
            jax.ShapeDtypeStruct((nb, NSTATE, C), F32),
        ),
        in_specs=[any_space, any_space],
        out_specs=(any_space, any_space),
        scratch_shapes=[dma((2,))],
        compiler_params=pltpu.CompilerParams(vmem_limit_bytes=4 * 1024 * 1024),
    )(on, returned)


def solution(mesh):
    in_specs = (
        P(("atm", "ocn"), None, None),
        P("ocn", None),
        P(("atm", "ocn")),
        P(("atm", "ocn"), None, None),
        P(),
        P(None, "atm", "ocn"),
        P("atm", "ocn"),
    )
    out_specs = (P(None, "atm", "ocn"), P(("atm", "ocn"), None, None))
    step = functools.partial(body, mesh.shape["atm"], mesh.shape["ocn"])
    return jax.shard_map(step, mesh=mesh, in_specs=in_specs, out_specs=out_specs, check_vma=False)
```

```python
import functools

import jax
import jax.numpy as jnp
from jax import lax
from jax.experimental import pallas as pl
from jax.experimental.pallas import tpu as pltpu
from jax.sharding import PartitionSpec as P

MESH = pl.DeviceIdType.MESH
F32 = jnp.float32
BF16 = jnp.bfloat16
NSTATE = 4
F = 16
C = 128
HIGHEST = lax.Precision.HIGHEST


def iota(shape, dim):
    return lax.broadcasted_iota(jnp.int32, shape, dim)


def split(x):
    high = x.astype(BF16).astype(F32)
    return jnp.concatenate([high, x - high], axis=0).astype(BF16)


def tend(x, lap, mask, state):
    rows = x.shape[0]
    rot = jnp.where(
        state == 0,
        pltpu.roll(x, rows - 1, 0),
        jnp.where(state == 1, -pltpu.roll(x, 1, 0), 0.0),
    )
    kappa = jnp.where(state < 2, F32(0.8), F32(0.5))
    return mask * (x + 0.25 * (kappa * lap + 0.5 * rot - 0.1 * x))


def kernel(
    na, no,
    atm_h, w_h, st_h, mk_h, cm_h, pat_h, c_h,
    on, returned,
    cm_v, cm_s, pat_s, c_v,
    atm, w32, whi, wlo, st, mk,
    out1, arr1, idx_s,
    row_out, row_in, col_out, col_in,
    mask_out, mask_in, a2_out, a2_in, a2_part, fix_out, fix_in,
    g, g_up, g_dn, gx, g_in, edge_out, edge_in, g_halo, back,
    in_sem, w_sem, x_send, x_recv, row_send, row_recv, col_send, col_recv, g_send, g_recv, h_send, h_recv,
):
    nb = na
    r4 = NSTATE * nb
    a = lax.axis_index("atm")
    o = lax.axis_index("ocn")
    line = a * no + o

    nz, nx = na // 4, no // 4
    zs = [lax.rem(lax.div(a, 4) + k, nz) * 4 for k in range(nz)]
    ys = [lax.rem(lax.rem(a, 4) + k, 4) for k in range(4)]
    xs = [lax.rem(lax.div(o, 4) + k, nx) * 4 for k in range(nx)]
    hs = [lax.rem(lax.div(o, 2) + k, 2) * 2 for k in range(2)]
    cs = [lax.rem(o + k, 2) for k in range(2)]
    z_order = [k for i in range(1, nz // 2 + 1) for k in ((nz - i, i) if nz - i != i else (i,))]
    atm_far = [zs[k] + ys[y] for k in z_order for y in (2, 1, 3, 0)]
    atm_near = [zs[0] + ys[y] for y in (2, 1, 3)]
    x_order = [nx // 2] + [k for k in range(nx) if k != nx // 2]
    ocn_far = [xs[k] + hs[1] + cs[c] for k in x_order for c in (1, 0)]
    ocn_near = [xs[k] + hs[0] + cs[c] for k in x_order for c in (1, 0) if k or c]
    atm_peers, ocn_peers = atm_far + atm_near, ocn_far + ocn_near

    barrier = pltpu.get_barrier_semaphore()

    def greet(device):
        pl.semaphore_signal(barrier, inc=1, device_id=device, device_id_type=MESH)

    for to in ocn_far:
        greet((a, to))
    for to in atm_far:
        greet((to, o))
    has_up, has_dn, has_left, has_right = a > 0, a < na - 1, o > 0, o < no - 1
    corners = []
    for dv, vert in ((-1, has_up), (1, has_dn)):
        @pl.when(vert)
        def _():
            greet((a + dv, no - 1 if dv < 0 else 0))

        for dh, hori in ((-1, has_left), (1, has_right)):
            corners.append((dv, dh, jnp.logical_and(vert, hori)))

            @pl.when(corners[-1][2])
            def _():
                greet((a + dv, o + dh))

    for to in ocn_near:
        greet((a, to))
    for to in atm_near:
        greet((to, o))
    first = jnp.logical_and(o == 0, has_up)
    last = jnp.logical_and(o == no - 1, has_dn)
    greetings = na + no - 2 + no * (first.astype(jnp.int32) + last.astype(jnp.int32))
    for _, _, there in corners:
        greetings += there.astype(jnp.int32)

    copies = [
        pltpu.make_async_copy(src, dst, in_sem.at[i])
        for i, (src, dst) in enumerate((
            (cm_h, cm_v), (c_h, c_v), (atm_h, atm), (st_h, st), (mk_h, mk), (cm_h, cm_s), (pat_h, pat_s)))
    ]
    for copy in copies:
        copy.start()
    for d in range(no):
        pltpu.make_async_copy(w_h.at[d], w32.at[d], w_sem.at[d]).start()

    copies[0].wait()
    copies[1].wait()
    slot = iota((r4, na * nb), 1)
    cm = cm_v[...]
    mine = jnp.where(cm // nb == a, (cm % nb).astype(F32), 0.0)
    mine = jnp.where(slot // nb == iota((r4, na * nb), 0) // NSTATE, mine, 0.0)
    order = jnp.sum(mine, axis=1, keepdims=True).astype(jnp.int32)
    coeff = c_v[...]
    coeff = jnp.concatenate([coeff] * 2, axis=0)
    coeff = jnp.concatenate([coeff] * (C // F), axis=1)
    coeff = jnp.concatenate([coeff] * (r4 // 8), axis=0)
    coeff = jnp.concatenate([coeff] * (nb * F // C), axis=1)
    take = jnp.where(order == iota((r4, nb * F), 1) // F, coeff, 0.0)
    copies[2].wait()
    states = jnp.dot(take, atm[...], precision=HIGHEST, preferred_element_type=F32)
    for b in range(nb):
        out1[b] = states[NSTATE * b : NSTATE * b + NSTATE]
    arr1[a] = out1[a]

    copies[3].wait()
    copies[4].wait()
    land = mk[...].astype(F32)
    for b in range(no):
        mask_out[b] = land[2 * b : 2 * b + 2]
    mask_in[o] = mask_out[o]
    for s in range(NSTATE):
        a2_out[pl.ds(s, nb, stride=NSTATE), :] = land
    wet = a2_out[...]
    for s in range(NSTATE):
        a2_out[pl.ds(s, nb, stride=NSTATE), :] = st[s]
    tile = a2_out[...]
    turned, wet_turned = tile.T, wet.T
    for i in range(2):
        row_out[0, i] = tile[NSTATE * i : NSTATE * i + NSTATE]
        row_out[1, i] = tile[r4 - NSTATE * i - NSTATE : r4 - NSTATE * i]
        col_out[0, i : i + 1] = turned[i : i + 1]
        col_out[1, i : i + 1] = turned[C - 1 - i : C - i]
    row_out[0, 2] = wet[:NSTATE]
    row_out[1, 2] = wet[r4 - NSTATE :]
    col_out[0, 2:3] = wet_turned[:1]
    col_out[1, 2:3] = wet_turned[C - 1 :]
    for side in range(2):
        col_out[side, 3:4] = jnp.zeros((1, r4), F32)

    def row_copy(side, up_or_down, target):
        return pltpu.make_async_remote_copy(
            row_out.at[side], row_in.at[up_or_down], row_send.at[side], row_recv.at[up_or_down],
            device_id=(target, o), device_id_type=MESH)

    def col_copy(side, place, flight, target):
        return pltpu.make_async_remote_copy(
            col_out.at[side], col_in.at[place], col_send.at[flight], col_recv.at[place],
            device_id=target, device_id_type=MESH)

    halos = [
        (has_left, col_copy(0, 3, 2, (a, o - 1)), col_copy(0, 2, 2, (a, o - 1))),
        (has_right, col_copy(1, 2, 3, (a, o + 1)), col_copy(1, 3, 3, (a, o + 1))),
    ]
    for dv, dh, there in corners:
        side = 0 if dh < 0 else 1
        here = (0 if dv < 0 else 4) + side
        halos.append((there, col_copy(side, 5 - here, here, (a + dv, o + dh)), col_copy(side, here, here, (a + dv, o + dh))))
    halos.append((has_up, row_copy(0, 1, a - 1), row_copy(0, 0, a - 1)))
    halos.append((has_dn, row_copy(1, 0, a + 1), row_copy(1, 1, a + 1)))

    for side, inside in ((0, has_up), (1, has_dn)):
        @pl.when(jnp.logical_not(inside))
        def _():
            row_in[side] = jnp.zeros((3, NSTATE, C), F32)
            g_halo[side] = jnp.zeros((NSTATE, C), F32)

    places = [(2, has_left), (3, has_right)]
    places += [((0 if dv < 0 else 4) + (0 if dh < 0 else 1), there) for dv, dh, there in corners]
    for place, inside in places:
        @pl.when(jnp.logical_not(inside))
        def _():
            col_in[place] = jnp.zeros((4, r4), F32)

    has_above, has_below = line > 0, line < na * no - 1

    @pl.when(jnp.logical_not(has_above))
    def _():
        g_up[...] = jnp.zeros_like(g_up)

    @pl.when(jnp.logical_not(has_below))
    def _():
        g_dn[...] = jnp.zeros_like(g_dn)

    def block_copy(to):
        return pltpu.make_async_remote_copy(
            out1.at[to], arr1.at[a], x_send.at[0], x_recv.at[0], device_id=(to, o), device_id_type=MESH)

    def ocn_copy(i, src, dst, to):
        return pltpu.make_async_remote_copy(
            src, dst, x_send.at[i], x_recv.at[i], device_id=(a, to), device_id_type=MESH)

    def rows_of(d):
        return pl.ds(pl.multiple_of(8 * d, 8), 8)

    def alone(x):
        lane, state = iota((r4, C), 1), iota((r4, C), 0) % NSTATE
        none = jnp.zeros((NSTATE, C), F32)
        up = jnp.concatenate([none, x[: r4 - NSTATE]], axis=0)
        down = jnp.concatenate([x[NSTATE:], none], axis=0)
        left = jnp.where(lane == 0, 0.0, pltpu.roll(x, 1, 1))
        right = jnp.where(lane == C - 1, 0.0, pltpu.roll(x, C - 1, 1))
        return tend(x, up + down + left + right - 4.0 * x, wet, state)

    a2_part[...] = alone(alone(tile))
    pl.semaphore_wait(barrier, greetings)
    for to in atm_far[: na // 2]:
        block_copy(to).start()
    for to in ocn_far:
        ocn_copy(1, mask_out.at[to], mask_in.at[o], to).start()
    for to in atm_far[na // 2 :] + atm_near:
        block_copy(to).start()
    for to in ocn_near:
        ocn_copy(1, mask_out.at[to], mask_in.at[o], to).start()
    for there, copy, _ in halos:
        @pl.when(there)
        def _():
            copy.start()

    copies[5].wait()
    copies[6].wait()
    for r in range(nb):
        idx_s[r] = cm_s[0, a * nb + pat_s[r]] // nb

    def split_weights(d, carry):
        pltpu.make_async_copy(w_h.at[d], w32.at[d], w_sem.at[d]).wait()
        w = w32[d]
        high = w.astype(BF16)
        whi[d] = high
        wlo[d] = (w - high.astype(F32)).astype(BF16)
        return carry

    lax.fori_loop(0, no, split_weights, 0)

    across = iota((r4, r4), 1)
    along = iota((r4, r4), 0)
    pattern = jnp.zeros((1, r4), jnp.int32)
    for r in range(nb):
        pattern = jnp.where(iota((1, r4), 1) // NSTATE == r, pat_s[r], pattern)
    place = jnp.logical_and(pattern == along // NSTATE, across % NSTATE == along % NSTATE)
    place = jnp.where(place, 1.0, 0.0).astype(BF16)

    def a2_copy(src, to):
        return ocn_copy(2, src.at[rows_of(to)], a2_in.at[rows_of(o)], to)

    def send_inner(to):
        @pl.when(jnp.logical_and(to > 0, to < no - 1))
        def _():
            a2_copy(a2_part, to).start()


    for there, _, copy in halos:
        @pl.when(there)
        def _():
            copy.wait_recv()

    for to in ocn_peers:
        send_inner(to)
    at, along_lane = iota((C, r4), 0), iota((C, r4), 1)
    beside = jnp.zeros((C, r4), F32)
    for i in range(3):
        beside = jnp.where(at == i, col_in[3, i : i + 1], beside)
        beside = jnp.where(at == C - 1 - i, col_in[2, i : i + 1], beside)
    diagonal = jnp.where(
        at == 0,
        jnp.where(along_lane < r4 // 2, col_in[5, :1], col_in[1, :1]),
        jnp.where(at == C - 1, jnp.where(along_lane < r4 // 2, col_in[4, :1], col_in[0, :1]), 0.0))
    beside, diagonal = beside.T, diagonal.T
    rows = r4 + 4 * NSTATE
    lane = iota((rows, C), 1)
    state = iota((rows, C), 0) % NSTATE
    none = jnp.zeros((NSTATE, C), F32)
    x = jnp.concatenate([row_in[0, 1], row_in[0, 0], tile, row_in[1, 0], row_in[1, 1]], axis=0)
    e = jnp.concatenate([none, diagonal[r4 - NSTATE :], beside, diagonal[:NSTATE], none], axis=0)
    wet_x = jnp.concatenate([none, row_in[0, 2], wet, row_in[1, 2], none], axis=0)
    wet_e = jnp.concatenate([none, none, beside, none, none], axis=0)
    wet_e = jnp.where(lane == 0, pltpu.roll(wet_e, C - 2, 1), jnp.where(lane == C - 1, pltpu.roll(wet_e, 2, 1), 0.0))

    def sides(x, e):
        x_right, e_right = pltpu.roll(x, 1, 1), pltpu.roll(e, 1, 1)
        x_left, e_left = pltpu.roll(x, C - 1, 1), pltpu.roll(e, C - 1, 1)
        low, high = iota(x.shape, 1) == 0, iota(x.shape, 1) == C - 1
        of_x = jnp.where(low, e_right, x_right) + jnp.where(high, e_left, x_left)
        of_e = jnp.where(low, x_right, e_right) + jnp.where(high, x_left, e_left)
        return of_x, of_e

    def rises(x):
        return pltpu.roll(x, NSTATE, 0) + pltpu.roll(x, rows - NSTATE, 0)

    of_x, of_e = sides(x, e)
    x, e = tend(x, rises(x) + of_x - 4.0 * x, wet_x, state), tend(e, rises(e) + of_e - 4.0 * e, wet_e, state)
    of_x, _ = sides(x, e)
    x = tend(x, rises(x) + of_x - 4.0 * x, wet_x, state)
    a2_out[...] = x[2 * NSTATE : 2 * NSTATE + r4]
    a2_in[rows_of(o)] = a2_out[rows_of(o)]
    for to in (0, no - 1):
        @pl.when(o != to)
        def _():
            a2_copy(a2_out, to).start()

    def by_pair(columns):
        lane, row = iota((r4, C), 1), iota((r4, C), 0) % 8
        found = jnp.zeros((r4, C), F32)
        for k, column in enumerate(columns):
            found = jnp.where(lane == row + 8 * k, column, found)
        return jnp.sum(found.reshape(no, 8, C), axis=1)

    def by_row(packed, k):
        lane, row = iota((r4, C), 1), iota((r4, C), 0) % 8
        return jnp.sum(jnp.where(lane == row + 8 * k, packed, 0.0), axis=1, keepdims=True)

    def spread(ref):
        return jnp.concatenate([jnp.broadcast_to(ref[d], (8, C)) for d in range(no)], axis=0)

    touched = (0, 1, C - 2, C - 1)
    added = a2_out[...] - a2_part[...]
    fix = by_pair([added[:, c : c + 1] for c in touched])
    for d in range(no):
        fix_out[d] = jnp.zeros((1, C), F32) if d in (0, no - 1) else fix[d : d + 1]
    fix_in[o] = jnp.zeros((1, C), F32)
    for to in ocn_peers:
        ocn_copy(5, fix_out.at[to], fix_in.at[o], to).start()

    def wait_all(i, ref, count, send):
        part = ref.at[pl.ds(0, count)]
        copy = ocn_copy(i, part, part, o)
        if send:
            copy.wait_send()
        else:
            copy.wait_recv()

    wait_all(1, mask_in, no - 1, False)
    wait_all(0, arr1, nb - 1, False)
    above = ((line - 1) // no, (line - 1) % no)
    below = ((line + 1) // no, (line + 1) % no)

    def g_copy(row, dst, place, target, part=None):
        src = g.at[row]
        if part is not None:
            src, dst = src.at[part], dst.at[part]
        return pltpu.make_async_remote_copy(
            src, dst, g_send.at[row], g_recv.at[place], device_id=target, device_id_type=MESH)

    def halo_copy(row, d, target):
        return pltpu.make_async_remote_copy(
            g.at[row, d], g_halo.at[1 - row], h_send.at[row], h_recv.at[1 - row],
            device_id=(target, d), device_id_type=MESH)

    pairs = []
    for q in range(no // 4):
        part = range(4 * q, 4 * q + 4)
        for d in part:
            x = split(jnp.concatenate([arr1[idx_s[2 * d]], arr1[idx_s[2 * d + 1]]], axis=1))
            f = jnp.dot(x, whi[d], preferred_element_type=F32) + jnp.dot(x, wlo[d], preferred_element_type=F32)
            f = 0.25 * (f[:NSTATE] + f[NSTATE:])
            pairs.append(jnp.concatenate([f[:, :C] * mask_in[d, 0:1], f[:, C:] * mask_in[d, 1:2]], axis=0))
        for d in part:
            gx[8 * d : 8 * d + 8] = pairs[d]
            g[0, d] = pairs[d][:NSTATE]
            g[1, d] = pairs[d][NSTATE:]
        here = pl.ds(4 * q, 4)

        @pl.when(has_above)
        def _():
            g_copy(0, g_dn, 1, above, here).start()

        @pl.when(has_below)
        def _():
            g_copy(1, g_up, 0, below, here).start()

        @pl.when(first)
        def _():
            for d in part:
                halo_copy(0, d, a - 1).start()

        @pl.when(last)
        def _():
            for d in part:
                halo_copy(1, d, a + 1).start()

        for d in part:
            @pl.when(o != d)
            def _():
                ocn_copy(3, gx.at[pl.ds(8 * d, 8)], g_in.at[rows_of(o)], d).start()

    g_in[rows_of(o)] = gx[rows_of(o)]

    whole = gx[...]
    one = jnp.zeros((8, 1), F32)
    edge = by_pair([
        jnp.concatenate([one, whole[: r4 - 8, C - 1 :]], axis=0),
        jnp.concatenate([whole[8:, :1], one], axis=0)])
    for d in range(no):
        edge_out[d] = edge[d : d + 1]
    for to in ocn_peers:
        ocn_copy(4, edge_out.at[to], edge_in.at[o], to).start()
    edge_in[o] = edge_out[o]
    lane8, row8 = iota((8, C), 1), iota((8, C), 0)
    nothing = jnp.zeros((8, C), F32)
    lefts = [pltpu.roll(x, 1, 1) for x in pairs]
    rights = [pltpu.roll(x, C - 1, 1) for x in pairs]

    wait_all(2, a2_in, 8 * (no - 1), False)
    wait_all(5, fix_in, no - 1, False)
    packed = spread(fix_in)
    x = a2_in[...]
    for k, c in enumerate(touched):
        x = x + jnp.where(iota((r4, C), 1) == c, by_row(packed, k), 0.0)
    a2_in[...] = x

    @pl.when(has_above)
    def _():
        g_copy(0, g_up, 0, above).wait_recv()

    @pl.when(has_below)
    def _():
        g_copy(1, g_dn, 1, below).wait_recv()

    nt = (((1,), (1,)), ((), ()))
    for d in range(no):
        x = pairs[d]
        up = jnp.concatenate([g_up[d], x[:NSTATE]], axis=0)
        down = jnp.concatenate([x[NSTATE:], g_dn[d]], axis=0)
        left = jnp.where(lane8 == 0, lefts[d - 1] if d > 0 else nothing, lefts[d])
        right = jnp.where(lane8 == C - 1, rights[d + 1] if d < no - 1 else nothing, rights[d])
        wet8 = jnp.where(row8 < NSTATE, mask_in[d, 0:1], mask_in[d, 1:2])
        x = a2_in[8 * d : 8 * d + 8] + (x + tend(x, up + down + left + right - 4.0 * x, wet8, row8 % NSTATE))
        x = split(jnp.concatenate([x[:NSTATE], x[NSTATE:]], axis=1))
        f = lax.dot_general(x, whi[d], nt, preferred_element_type=F32) + lax.dot_general(
            x, wlo[d], nt, preferred_element_type=F32)
        f = f[:NSTATE] + f[NSTATE:]
        back[8 * d : 8 * d + 8] = jnp.concatenate([f[:, :C], f[:, C:]], axis=0)

    x = back[...]
    high = x.astype(BF16)
    rest = x - high.astype(F32)
    middle = rest.astype(BF16)
    low = (rest - middle.astype(F32)).astype(BF16)
    placed = jnp.dot(place, jnp.concatenate([high, middle, low], axis=1), preferred_element_type=F32)
    placed = placed[:, :C] + placed[:, C : 2 * C] + placed[:, 2 * C :]
    for b in range(nb):
        returned[b] = placed[NSTATE * b : NSTATE * b + NSTATE]

    wait_all(3, g_in, 8 * (no - 1), False)
    wait_all(4, edge_in, no - 1, False)

    @pl.when(has_up)
    def _():
        halo_copy(1, 0, a).wait_recv()

    @pl.when(has_dn)
    def _():
        halo_copy(0, 0, a).wait_recv()

    x = g_in[...]
    edge = spread(edge_in)
    lane, row = iota((r4, C), 1), iota((r4, C), 0)
    before, after = by_row(edge, 0), by_row(edge, 1)
    up = jnp.concatenate([g_halo[0], x[: r4 - NSTATE]], axis=0)
    down = jnp.concatenate([x[NSTATE:], g_halo[1]], axis=0)
    left = jnp.where(lane == 0, before, pltpu.roll(x, 1, 1))
    right = jnp.where(lane == C - 1, after, pltpu.roll(x, C - 1, 1))
    back[...] = a2_out[...] + (x + tend(x, up + down + left + right - 4.0 * x, wet, row % NSTATE))
    for s in range(NSTATE):
        on[s] = back[pl.ds(s, nb, stride=NSTATE), :]

    wait_all(0, out1, nb - 1, True)
    wait_all(1, mask_out, no - 1, True)
    wait_all(2, a2_out, 8 * (no - 1), True)
    wait_all(3, gx, 8 * (no - 1), True)
    wait_all(4, edge_out, no - 1, True)
    wait_all(5, fix_out, no - 1, True)
    for there, copy, _ in halos:
        @pl.when(there)
        def _():
            copy.wait_send()

    @pl.when(has_above)
    def _():
        g_copy(0, g_dn, 1, above).wait_send()

    @pl.when(has_below)
    def _():
        g_copy(1, g_up, 0, below).wait_send()

    for row, sends in ((0, first), (1, last)):
        @pl.when(sends)
        def _():
            pltpu.make_async_remote_copy(
                g.at[row], g_up, h_send.at[row], h_recv.at[1 - row], device_id=(a, o), device_id_type=MESH).wait_send()


def finish(on, returned, on_h, returned_h, sems):
    copies = [pltpu.make_async_copy(on, on_h, sems.at[0]), pltpu.make_async_copy(returned, returned_h, sems.at[1])]
    for copy in copies:
        copy.start()
    for copy in copies:
        copy.wait()


def body(na, no, atm_fields, coupler_map, remap_pattern, remap_weights, bulk_coeffs, ocean_state, land_mask):
    nb = atm_fields.shape[0]
    r4 = NSTATE * nb
    any_space = pl.BlockSpec(memory_space=pl.ANY)
    vmem = pl.BlockSpec(memory_space=pltpu.VMEM)
    dma = pltpu.SemaphoreType.DMA
    on, returned = pl.pallas_call(
        functools.partial(kernel, na, no),
        out_shape=(pltpu.VMEM((NSTATE, nb, C), F32), pltpu.VMEM((nb, NSTATE, C), F32)),
        in_specs=[any_space] * 7,
        out_specs=(vmem, vmem),
        scratch_shapes=[
            pltpu.VMEM((1, na * nb), jnp.int32),
            pltpu.SMEM((1, na * nb), jnp.int32),
            pltpu.SMEM((nb,), jnp.int32),
            pltpu.VMEM((NSTATE, F), F32),
            pltpu.VMEM((nb * F, C), F32),
            pltpu.VMEM((no, 2 * C, 2 * C), F32),
            pltpu.VMEM((no, 2 * C, 2 * C), BF16),
            pltpu.VMEM((no, 2 * C, 2 * C), BF16),
            pltpu.VMEM((NSTATE, nb, C), F32),
            pltpu.VMEM((nb, C), jnp.int32),
            pltpu.VMEM((nb, NSTATE, C), F32),
            pltpu.VMEM((nb, NSTATE, C), F32),
            pltpu.SMEM((nb,), jnp.int32),
            pltpu.VMEM((2, 3, NSTATE, C), F32),
            pltpu.VMEM((2, 3, NSTATE, C), F32),
            pltpu.VMEM((2, 4, r4), F32),
            pltpu.VMEM((6, 4, r4), F32),
            pltpu.VMEM((no, 2, C), F32),
            pltpu.VMEM((no, 2, C), F32),
            pltpu.VMEM((r4, C), F32),
            pltpu.VMEM((r4, C), F32),
            pltpu.VMEM((r4, C), F32),
            pltpu.VMEM((no, 1, C), F32),
            pltpu.VMEM((no, 1, C), F32),
            pltpu.VMEM((2, no, NSTATE, C), F32),
            pltpu.VMEM((no, NSTATE, C), F32),
            pltpu.VMEM((no, NSTATE, C), F32),
            pltpu.VMEM((r4, C), F32),
            pltpu.VMEM((r4, C), F32),
            pltpu.VMEM((no, 1, C), F32),
            pltpu.VMEM((no, 1, C), F32),
            pltpu.VMEM((2, NSTATE, C), F32),
            pltpu.VMEM((r4, C), F32),
            dma((7,)),
            dma((no,)),
            dma((6,)),
            dma((6,)),
            dma((2,)),
            dma((2,)),
            dma((6,)),
            dma((6,)),
            dma((2,)),
            dma((2,)),
            dma((2,)),
            dma((2,)),
        ],
        compiler_params=pltpu.CompilerParams(
            collective_id=0, has_side_effects=True, vmem_limit_bytes=60 * 1024 * 1024
        ),
    )(
        atm_fields.reshape(nb * F, C),
        remap_weights.reshape(no, 2 * C, 2 * C),
        ocean_state,
        land_mask,
        coupler_map,
        remap_pattern,
        bulk_coeffs,
    )
    return pl.pallas_call(
        finish,
        out_shape=(
            jax.ShapeDtypeStruct(ocean_state.shape, F32),
            jax.ShapeDtypeStruct((nb, NSTATE, C), F32),
        ),
        in_specs=[any_space, any_space],
        out_specs=(any_space, any_space),
        scratch_shapes=[dma((2,))],
        compiler_params=pltpu.CompilerParams(vmem_limit_bytes=4 * 1024 * 1024),
    )(on, returned)


def solution(mesh):
    in_specs = (
        P(("atm", "ocn"), None, None),
        P("ocn", None),
        P(("atm", "ocn")),
        P(("atm", "ocn"), None, None),
        P(),
        P(None, "atm", "ocn"),
        P("atm", "ocn"),
    )
    out_specs = (P(None, "atm", "ocn"), P(("atm", "ocn"), None, None))
    step = functools.partial(body, mesh.shape["atm"], mesh.shape["ocn"])
    return jax.shard_map(step, mesh=mesh, in_specs=in_specs, out_specs=out_specs, check_vma=False)
```

```python
import functools

import jax
import jax.numpy as jnp
from jax import lax
from jax.experimental import pallas as pl
from jax.experimental.pallas import tpu as pltpu
from jax.sharding import PartitionSpec as P

MESH = pl.DeviceIdType.MESH
F32 = jnp.float32
BF16 = jnp.bfloat16
NSTATE = 4
F = 16
C = 128
HIGHEST = lax.Precision.HIGHEST


def iota(shape, dim):
    return lax.broadcasted_iota(jnp.int32, shape, dim)


def split(x):
    high = x.astype(BF16).astype(F32)
    return jnp.concatenate([high, x - high], axis=0).astype(BF16)


def tend(x, lap, mask, state):
    rows = x.shape[0]
    rot = jnp.where(
        state == 0,
        pltpu.roll(x, rows - 1, 0),
        jnp.where(state == 1, -pltpu.roll(x, 1, 0), 0.0),
    )
    kappa = jnp.where(state < 2, F32(0.8), F32(0.5))
    return mask * (x + 0.25 * (kappa * lap + 0.5 * rot - 0.1 * x))


def kernel(
    na, no,
    atm_h, w_h, st_h, mk_h, cm_h, pat_h, c_h,
    on, returned,
    cm_v, cm_s, pat_s, c_v,
    atm, w32, whi, wlo, st, mk,
    out1, arr1, idx_s,
    row_out, row_in, col_out, col_in,
    mask_out, mask_in, a2_out, a2_in, a2_part, fix_out, fix_in,
    g, g_up, g_dn, gx, g_in, edge_out, edge_in, g_halo, back,
    in_sem, w_sem, x_send, x_recv, row_send, row_recv, col_send, col_recv, g_send, g_recv, h_send, h_recv,
):
    nb = na
    r4 = NSTATE * nb
    a = lax.axis_index("atm")
    o = lax.axis_index("ocn")
    line = a * no + o

    nz, nx = na // 4, no // 4
    zs = [lax.rem(lax.div(a, 4) + k, nz) * 4 for k in range(nz)]
    ys = [lax.rem(lax.rem(a, 4) + k, 4) for k in range(4)]
    xs = [lax.rem(lax.div(o, 4) + k, nx) * 4 for k in range(nx)]
    hs = [lax.rem(lax.div(o, 2) + k, 2) * 2 for k in range(2)]
    cs = [lax.rem(o + k, 2) for k in range(2)]
    z_order = [k for i in range(1, nz // 2 + 1) for k in ((nz - i, i) if nz - i != i else (i,))]
    atm_far = [zs[k] + ys[y] for k in z_order for y in (2, 1, 3, 0)]
    atm_near = [zs[0] + ys[y] for y in (2, 1, 3)]
    x_order = [nx // 2] + [k for k in range(nx) if k != nx // 2]
    ocn_far = [xs[k] + hs[1] + cs[c] for k in x_order for c in (1, 0)]
    ocn_near = [xs[k] + hs[0] + cs[c] for k in x_order for c in (1, 0) if k or c]
    atm_peers, ocn_peers = atm_far + atm_near, ocn_far + ocn_near

    barrier = pltpu.get_barrier_semaphore()

    def greet(device):
        pl.semaphore_signal(barrier, inc=1, device_id=device, device_id_type=MESH)

    for to in ocn_far:
        greet((a, to))
    for to in atm_far:
        greet((to, o))
    has_up, has_dn, has_left, has_right = a > 0, a < na - 1, o > 0, o < no - 1
    corners = []
    for dv, vert in ((-1, has_up), (1, has_dn)):
        @pl.when(vert)
        def _():
            greet((a + dv, no - 1 if dv < 0 else 0))

        for dh, hori in ((-1, has_left), (1, has_right)):
            corners.append((dv, dh, jnp.logical_and(vert, hori)))

            @pl.when(corners[-1][2])
            def _():
                greet((a + dv, o + dh))

    for to in ocn_near:
        greet((a, to))
    for to in atm_near:
        greet((to, o))
    first = jnp.logical_and(o == 0, has_up)
    last = jnp.logical_and(o == no - 1, has_dn)
    greetings = na + no - 2 + no * (first.astype(jnp.int32) + last.astype(jnp.int32))
    for _, _, there in corners:
        greetings += there.astype(jnp.int32)

    copies = [
        pltpu.make_async_copy(src, dst, in_sem.at[i])
        for i, (src, dst) in enumerate((
            (cm_h, cm_v), (c_h, c_v), (atm_h, atm), (st_h, st), (mk_h, mk), (cm_h, cm_s), (pat_h, pat_s)))
    ]
    for copy in copies:
        copy.start()
    for d in range(no):
        pltpu.make_async_copy(w_h.at[d], w32.at[d], w_sem.at[d]).start()

    copies[0].wait()
    copies[1].wait()
    slot = iota((r4, na * nb), 1)
    cm = cm_v[...]
    mine = jnp.where(cm // nb == a, (cm % nb).astype(F32), 0.0)
    mine = jnp.where(slot // nb == iota((r4, na * nb), 0) // NSTATE, mine, 0.0)
    order = jnp.sum(mine, axis=1, keepdims=True).astype(jnp.int32)
    coeff = c_v[...]
    coeff = jnp.concatenate([coeff] * 2, axis=0)
    coeff = jnp.concatenate([coeff] * (C // F), axis=1)
    coeff = jnp.concatenate([coeff] * (r4 // 8), axis=0)
    coeff = jnp.concatenate([coeff] * (nb * F // C), axis=1)
    take = jnp.where(order == iota((r4, nb * F), 1) // F, coeff, 0.0)
    copies[2].wait()
    states = jnp.dot(take, atm[...], precision=HIGHEST, preferred_element_type=F32)
    for b in range(nb):
        out1[b] = states[NSTATE * b : NSTATE * b + NSTATE]
    arr1[a] = out1[a]

    copies[3].wait()
    copies[4].wait()
    land = mk[...].astype(F32)
    for b in range(no):
        mask_out[b] = land[2 * b : 2 * b + 2]
    mask_in[o] = mask_out[o]
    for s in range(NSTATE):
        a2_out[pl.ds(s, nb, stride=NSTATE), :] = land
    wet = a2_out[...]
    for s in range(NSTATE):
        a2_out[pl.ds(s, nb, stride=NSTATE), :] = st[s]
    tile = a2_out[...]
    turned, wet_turned = tile.T, wet.T
    for i in range(2):
        row_out[0, i] = tile[NSTATE * i : NSTATE * i + NSTATE]
        row_out[1, i] = tile[r4 - NSTATE * i - NSTATE : r4 - NSTATE * i]
        col_out[0, i : i + 1] = turned[i : i + 1]
        col_out[1, i : i + 1] = turned[C - 1 - i : C - i]
    row_out[0, 2] = wet[:NSTATE]
    row_out[1, 2] = wet[r4 - NSTATE :]
    col_out[0, 2:3] = wet_turned[:1]
    col_out[1, 2:3] = wet_turned[C - 1 :]
    for side in range(2):
        col_out[side, 3:4] = jnp.zeros((1, r4), F32)

    def row_copy(side, up_or_down, target):
        return pltpu.make_async_remote_copy(
            row_out.at[side], row_in.at[up_or_down], row_send.at[side], row_recv.at[up_or_down],
            device_id=(target, o), device_id_type=MESH)

    def col_copy(side, place, flight, target):
        return pltpu.make_async_remote_copy(
            col_out.at[side], col_in.at[place], col_send.at[flight], col_recv.at[place],
            device_id=target, device_id_type=MESH)

    halos = [
        (has_left, col_copy(0, 3, 2, (a, o - 1)), col_copy(0, 2, 2, (a, o - 1))),
        (has_right, col_copy(1, 2, 3, (a, o + 1)), col_copy(1, 3, 3, (a, o + 1))),
    ]
    for dv, dh, there in corners:
        side = 0 if dh < 0 else 1
        here = (0 if dv < 0 else 4) + side
        halos.append((there, col_copy(side, 5 - here, here, (a + dv, o + dh)), col_copy(side, here, here, (a + dv, o + dh))))
    halos.append((has_up, row_copy(0, 1, a - 1), row_copy(0, 0, a - 1)))
    halos.append((has_dn, row_copy(1, 0, a + 1), row_copy(1, 1, a + 1)))

    for side, inside in ((0, has_up), (1, has_dn)):
        @pl.when(jnp.logical_not(inside))
        def _():
            row_in[side] = jnp.zeros((3, NSTATE, C), F32)
            g_halo[side] = jnp.zeros((NSTATE, C), F32)

    places = [(2, has_left), (3, has_right)]
    places += [((0 if dv < 0 else 4) + (0 if dh < 0 else 1), there) for dv, dh, there in corners]
    for place, inside in places:
        @pl.when(jnp.logical_not(inside))
        def _():
            col_in[place] = jnp.zeros((4, r4), F32)

    has_above, has_below = line > 0, line < na * no - 1

    @pl.when(jnp.logical_not(has_above))
    def _():
        g_up[...] = jnp.zeros_like(g_up)

    @pl.when(jnp.logical_not(has_below))
    def _():
        g_dn[...] = jnp.zeros_like(g_dn)

    def block_copy(to):
        return pltpu.make_async_remote_copy(
            out1.at[to], arr1.at[a], x_send.at[0], x_recv.at[0], device_id=(to, o), device_id_type=MESH)

    def ocn_copy(i, src, dst, to):
        return pltpu.make_async_remote_copy(
            src, dst, x_send.at[i], x_recv.at[i], device_id=(a, to), device_id_type=MESH)

    def rows_of(d):
        return pl.ds(pl.multiple_of(8 * d, 8), 8)

    def alone(x):
        lane, state = iota((r4, C), 1), iota((r4, C), 0) % NSTATE
        none = jnp.zeros((NSTATE, C), F32)
        up = jnp.concatenate([none, x[: r4 - NSTATE]], axis=0)
        down = jnp.concatenate([x[NSTATE:], none], axis=0)
        left = jnp.where(lane == 0, 0.0, pltpu.roll(x, 1, 1))
        right = jnp.where(lane == C - 1, 0.0, pltpu.roll(x, C - 1, 1))
        return tend(x, up + down + left + right - 4.0 * x, wet, state)

    a2_part[...] = alone(alone(tile))
    pl.semaphore_wait(barrier, greetings)
    for to in atm_far[: na // 2]:
        block_copy(to).start()
    for to in ocn_far:
        ocn_copy(1, mask_out.at[to], mask_in.at[o], to).start()
    for to in atm_far[na // 2 :] + atm_near:
        block_copy(to).start()
    for to in ocn_near:
        ocn_copy(1, mask_out.at[to], mask_in.at[o], to).start()
    for there, copy, _ in halos:
        @pl.when(there)
        def _():
            copy.start()

    copies[5].wait()
    copies[6].wait()
    for r in range(nb):
        idx_s[r] = cm_s[0, a * nb + pat_s[r]] // nb

    def split_weights(d, carry):
        pltpu.make_async_copy(w_h.at[d], w32.at[d], w_sem.at[d]).wait()
        w = w32[d]
        high = w.astype(BF16)
        whi[d] = high
        wlo[d] = (w - high.astype(F32)).astype(BF16)
        return carry

    lax.fori_loop(0, no, split_weights, 0)

    across = iota((r4, r4), 1)
    along = iota((r4, r4), 0)
    pattern = jnp.zeros((1, r4), jnp.int32)
    for r in range(nb):
        pattern = jnp.where(iota((1, r4), 1) // NSTATE == r, pat_s[r], pattern)
    place = jnp.logical_and(pattern == along // NSTATE, across % NSTATE == along % NSTATE)
    place = jnp.where(place, 1.0, 0.0).astype(BF16)

    def a2_copy(src, to):
        return ocn_copy(2, src.at[rows_of(to)], a2_in.at[rows_of(o)], to)

    def send_inner(to):
        @pl.when(jnp.logical_and(to > 0, to < no - 1))
        def _():
            a2_copy(a2_part, to).start()


    for to in ocn_near:
        send_inner(to)

    for there, _, copy in halos:
        @pl.when(there)
        def _():
            copy.wait_recv()

    for to in ocn_far:
        send_inner(to)
    at, along_lane = iota((C, r4), 0), iota((C, r4), 1)
    beside = jnp.zeros((C, r4), F32)
    for i in range(3):
        beside = jnp.where(at == i, col_in[3, i : i + 1], beside)
        beside = jnp.where(at == C - 1 - i, col_in[2, i : i + 1], beside)
    diagonal = jnp.where(
        at == 0,
        jnp.where(along_lane < r4 // 2, col_in[5, :1], col_in[1, :1]),
        jnp.where(at == C - 1, jnp.where(along_lane < r4 // 2, col_in[4, :1], col_in[0, :1]), 0.0))
    beside, diagonal = beside.T, diagonal.T
    rows = r4 + 4 * NSTATE
    lane = iota((rows, C), 1)
    state = iota((rows, C), 0) % NSTATE
    none = jnp.zeros((NSTATE, C), F32)
    x = jnp.concatenate([row_in[0, 1], row_in[0, 0], tile, row_in[1, 0], row_in[1, 1]], axis=0)
    e = jnp.concatenate([none, diagonal[r4 - NSTATE :], beside, diagonal[:NSTATE], none], axis=0)
    wet_x = jnp.concatenate([none, row_in[0, 2], wet, row_in[1, 2], none], axis=0)
    wet_e = jnp.concatenate([none, none, beside, none, none], axis=0)
    wet_e = jnp.where(lane == 0, pltpu.roll(wet_e, C - 2, 1), jnp.where(lane == C - 1, pltpu.roll(wet_e, 2, 1), 0.0))

    def sides(x, e):
        x_right, e_right = pltpu.roll(x, 1, 1), pltpu.roll(e, 1, 1)
        x_left, e_left = pltpu.roll(x, C - 1, 1), pltpu.roll(e, C - 1, 1)
        low, high = iota(x.shape, 1) == 0, iota(x.shape, 1) == C - 1
        of_x = jnp.where(low, e_right, x_right) + jnp.where(high, e_left, x_left)
        of_e = jnp.where(low, x_right, e_right) + jnp.where(high, x_left, e_left)
        return of_x, of_e

    def rises(x):
        return pltpu.roll(x, NSTATE, 0) + pltpu.roll(x, rows - NSTATE, 0)

    of_x, of_e = sides(x, e)
    x, e = tend(x, rises(x) + of_x - 4.0 * x, wet_x, state), tend(e, rises(e) + of_e - 4.0 * e, wet_e, state)
    of_x, _ = sides(x, e)
    x = tend(x, rises(x) + of_x - 4.0 * x, wet_x, state)
    a2_out[...] = x[2 * NSTATE : 2 * NSTATE + r4]
    a2_in[rows_of(o)] = a2_out[rows_of(o)]
    for to in (0, no - 1):
        @pl.when(o != to)
        def _():
            a2_copy(a2_out, to).start()

    def by_pair(columns):
        lane, row = iota((r4, C), 1), iota((r4, C), 0) % 8
        found = jnp.zeros((r4, C), F32)
        for k, column in enumerate(columns):
            found = jnp.where(lane == row + 8 * k, column, found)
        return jnp.sum(found.reshape(no, 8, C), axis=1)

    def by_row(packed, k):
        lane, row = iota((r4, C), 1), iota((r4, C), 0) % 8
        return jnp.sum(jnp.where(lane == row + 8 * k, packed, 0.0), axis=1, keepdims=True)

    def spread(ref):
        return jnp.concatenate([jnp.broadcast_to(ref[d], (8, C)) for d in range(no)], axis=0)

    touched = (0, 1, C - 2, C - 1)
    added = a2_out[...] - a2_part[...]
    fix = by_pair([added[:, c : c + 1] for c in touched])
    for d in range(no):
        fix_out[d] = jnp.zeros((1, C), F32) if d in (0, no - 1) else fix[d : d + 1]
    fix_in[o] = jnp.zeros((1, C), F32)
    for to in ocn_peers:
        ocn_copy(5, fix_out.at[to], fix_in.at[o], to).start()

    def wait_all(i, ref, count, send):
        part = ref.at[pl.ds(0, count)]
        copy = ocn_copy(i, part, part, o)
        if send:
            copy.wait_send()
        else:
            copy.wait_recv()

    wait_all(1, mask_in, no - 1, False)
    wait_all(0, arr1, nb - 1, False)
    above = ((line - 1) // no, (line - 1) % no)
    below = ((line + 1) // no, (line + 1) % no)

    def g_copy(row, dst, place, target, part=None):
        src = g.at[row]
        if part is not None:
            src, dst = src.at[part], dst.at[part]
        return pltpu.make_async_remote_copy(
            src, dst, g_send.at[row], g_recv.at[place], device_id=target, device_id_type=MESH)

    def halo_copy(row, d, target):
        return pltpu.make_async_remote_copy(
            g.at[row, d], g_halo.at[1 - row], h_send.at[row], h_recv.at[1 - row],
            device_id=(target, d), device_id_type=MESH)

    pairs = []
    for q in range(no // 4):
        part = range(4 * q, 4 * q + 4)
        for d in part:
            x = split(jnp.concatenate([arr1[idx_s[2 * d]], arr1[idx_s[2 * d + 1]]], axis=1))
            f = jnp.dot(x, whi[d], preferred_element_type=F32) + jnp.dot(x, wlo[d], preferred_element_type=F32)
            f = 0.25 * (f[:NSTATE] + f[NSTATE:])
            pairs.append(jnp.concatenate([f[:, :C] * mask_in[d, 0:1], f[:, C:] * mask_in[d, 1:2]], axis=0))
        for d in part:
            gx[8 * d : 8 * d + 8] = pairs[d]
            g[0, d] = pairs[d][:NSTATE]
            g[1, d] = pairs[d][NSTATE:]
        here = pl.ds(4 * q, 4)

        @pl.when(has_above)
        def _():
            g_copy(0, g_dn, 1, above, here).start()

        @pl.when(has_below)
        def _():
            g_copy(1, g_up, 0, below, here).start()

        @pl.when(first)
        def _():
            for d in part:
                halo_copy(0, d, a - 1).start()

        @pl.when(last)
        def _():
            for d in part:
                halo_copy(1, d, a + 1).start()

        for apart in (True, False):
            for d in part:
                far = lax.rem(lax.div(o, 2), 2) != d // 2 % 2

                @pl.when(far if apart else jnp.logical_and(jnp.logical_not(far), o != d))
                def _():
                    ocn_copy(3, gx.at[pl.ds(8 * d, 8)], g_in.at[rows_of(o)], d).start()

    g_in[rows_of(o)] = gx[rows_of(o)]

    whole = gx[...]
    one = jnp.zeros((8, 1), F32)
    edge = by_pair([
        jnp.concatenate([one, whole[: r4 - 8, C - 1 :]], axis=0),
        jnp.concatenate([whole[8:, :1], one], axis=0)])
    for d in range(no):
        edge_out[d] = edge[d : d + 1]
    for to in ocn_peers:
        ocn_copy(4, edge_out.at[to], edge_in.at[o], to).start()
    edge_in[o] = edge_out[o]
    lane8, row8 = iota((8, C), 1), iota((8, C), 0)
    nothing = jnp.zeros((8, C), F32)
    lefts = [pltpu.roll(x, 1, 1) for x in pairs]
    rights = [pltpu.roll(x, C - 1, 1) for x in pairs]

    wait_all(2, a2_in, 8 * (no - 1), False)
    wait_all(5, fix_in, no - 1, False)
    packed = spread(fix_in)
    x = a2_in[...]
    for k, c in enumerate(touched):
        x = x + jnp.where(iota((r4, C), 1) == c, by_row(packed, k), 0.0)
    a2_in[...] = x

    @pl.when(has_above)
    def _():
        g_copy(0, g_up, 0, above).wait_recv()

    @pl.when(has_below)
    def _():
        g_copy(1, g_dn, 1, below).wait_recv()

    nt = (((1,), (1,)), ((), ()))
    for d in range(no):
        x = pairs[d]
        up = jnp.concatenate([g_up[d], x[:NSTATE]], axis=0)
        down = jnp.concatenate([x[NSTATE:], g_dn[d]], axis=0)
        left = jnp.where(lane8 == 0, lefts[d - 1] if d > 0 else nothing, lefts[d])
        right = jnp.where(lane8 == C - 1, rights[d + 1] if d < no - 1 else nothing, rights[d])
        wet8 = jnp.where(row8 < NSTATE, mask_in[d, 0:1], mask_in[d, 1:2])
        x = a2_in[8 * d : 8 * d + 8] + (x + tend(x, up + down + left + right - 4.0 * x, wet8, row8 % NSTATE))
        x = split(jnp.concatenate([x[:NSTATE], x[NSTATE:]], axis=1))
        f = lax.dot_general(x, whi[d], nt, preferred_element_type=F32) + lax.dot_general(
            x, wlo[d], nt, preferred_element_type=F32)
        f = f[:NSTATE] + f[NSTATE:]
        back[8 * d : 8 * d + 8] = jnp.concatenate([f[:, :C], f[:, C:]], axis=0)

    x = back[...]
    high = x.astype(BF16)
    rest = x - high.astype(F32)
    middle = rest.astype(BF16)
    low = (rest - middle.astype(F32)).astype(BF16)
    placed = jnp.dot(place, jnp.concatenate([high, middle, low], axis=1), preferred_element_type=F32)
    placed = placed[:, :C] + placed[:, C : 2 * C] + placed[:, 2 * C :]
    for b in range(nb):
        returned[b] = placed[NSTATE * b : NSTATE * b + NSTATE]

    wait_all(3, g_in, 8 * (no - 1), False)
    wait_all(4, edge_in, no - 1, False)

    @pl.when(has_up)
    def _():
        halo_copy(1, 0, a).wait_recv()

    @pl.when(has_dn)
    def _():
        halo_copy(0, 0, a).wait_recv()

    x = g_in[...]
    edge = spread(edge_in)
    lane, row = iota((r4, C), 1), iota((r4, C), 0)
    before, after = by_row(edge, 0), by_row(edge, 1)
    up = jnp.concatenate([g_halo[0], x[: r4 - NSTATE]], axis=0)
    down = jnp.concatenate([x[NSTATE:], g_halo[1]], axis=0)
    left = jnp.where(lane == 0, before, pltpu.roll(x, 1, 1))
    right = jnp.where(lane == C - 1, after, pltpu.roll(x, C - 1, 1))
    back[...] = a2_out[...] + (x + tend(x, up + down + left + right - 4.0 * x, wet, row % NSTATE))
    for s in range(NSTATE):
        on[s] = back[pl.ds(s, nb, stride=NSTATE), :]

    wait_all(0, out1, nb - 1, True)
    wait_all(1, mask_out, no - 1, True)
    wait_all(2, a2_out, 8 * (no - 1), True)
    wait_all(3, gx, 8 * (no - 1), True)
    wait_all(4, edge_out, no - 1, True)
    wait_all(5, fix_out, no - 1, True)
    for there, copy, _ in halos:
        @pl.when(there)
        def _():
            copy.wait_send()

    @pl.when(has_above)
    def _():
        g_copy(0, g_dn, 1, above).wait_send()

    @pl.when(has_below)
    def _():
        g_copy(1, g_up, 0, below).wait_send()

    for row, sends in ((0, first), (1, last)):
        @pl.when(sends)
        def _():
            pltpu.make_async_remote_copy(
                g.at[row], g_up, h_send.at[row], h_recv.at[1 - row], device_id=(a, o), device_id_type=MESH).wait_send()


def finish(on, returned, on_h, returned_h, sems):
    copies = [pltpu.make_async_copy(on, on_h, sems.at[0]), pltpu.make_async_copy(returned, returned_h, sems.at[1])]
    for copy in copies:
        copy.start()
    for copy in copies:
        copy.wait()


def body(na, no, atm_fields, coupler_map, remap_pattern, remap_weights, bulk_coeffs, ocean_state, land_mask):
    nb = atm_fields.shape[0]
    r4 = NSTATE * nb
    any_space = pl.BlockSpec(memory_space=pl.ANY)
    vmem = pl.BlockSpec(memory_space=pltpu.VMEM)
    dma = pltpu.SemaphoreType.DMA
    on, returned = pl.pallas_call(
        functools.partial(kernel, na, no),
        out_shape=(pltpu.VMEM((NSTATE, nb, C), F32), pltpu.VMEM((nb, NSTATE, C), F32)),
        in_specs=[any_space] * 7,
        out_specs=(vmem, vmem),
        scratch_shapes=[
            pltpu.VMEM((1, na * nb), jnp.int32),
            pltpu.SMEM((1, na * nb), jnp.int32),
            pltpu.SMEM((nb,), jnp.int32),
            pltpu.VMEM((NSTATE, F), F32),
            pltpu.VMEM((nb * F, C), F32),
            pltpu.VMEM((no, 2 * C, 2 * C), F32),
            pltpu.VMEM((no, 2 * C, 2 * C), BF16),
            pltpu.VMEM((no, 2 * C, 2 * C), BF16),
            pltpu.VMEM((NSTATE, nb, C), F32),
            pltpu.VMEM((nb, C), jnp.int32),
            pltpu.VMEM((nb, NSTATE, C), F32),
            pltpu.VMEM((nb, NSTATE, C), F32),
            pltpu.SMEM((nb,), jnp.int32),
            pltpu.VMEM((2, 3, NSTATE, C), F32),
            pltpu.VMEM((2, 3, NSTATE, C), F32),
            pltpu.VMEM((2, 4, r4), F32),
            pltpu.VMEM((6, 4, r4), F32),
            pltpu.VMEM((no, 2, C), F32),
            pltpu.VMEM((no, 2, C), F32),
            pltpu.VMEM((r4, C), F32),
            pltpu.VMEM((r4, C), F32),
            pltpu.VMEM((r4, C), F32),
            pltpu.VMEM((no, 1, C), F32),
            pltpu.VMEM((no, 1, C), F32),
            pltpu.VMEM((2, no, NSTATE, C), F32),
            pltpu.VMEM((no, NSTATE, C), F32),
            pltpu.VMEM((no, NSTATE, C), F32),
            pltpu.VMEM((r4, C), F32),
            pltpu.VMEM((r4, C), F32),
            pltpu.VMEM((no, 1, C), F32),
            pltpu.VMEM((no, 1, C), F32),
            pltpu.VMEM((2, NSTATE, C), F32),
            pltpu.VMEM((r4, C), F32),
            dma((7,)),
            dma((no,)),
            dma((6,)),
            dma((6,)),
            dma((2,)),
            dma((2,)),
            dma((6,)),
            dma((6,)),
            dma((2,)),
            dma((2,)),
            dma((2,)),
            dma((2,)),
        ],
        compiler_params=pltpu.CompilerParams(
            collective_id=0, has_side_effects=True, vmem_limit_bytes=60 * 1024 * 1024
        ),
    )(
        atm_fields.reshape(nb * F, C),
        remap_weights.reshape(no, 2 * C, 2 * C),
        ocean_state,
        land_mask,
        coupler_map,
        remap_pattern,
        bulk_coeffs,
    )
    return pl.pallas_call(
        finish,
        out_shape=(
            jax.ShapeDtypeStruct(ocean_state.shape, F32),
            jax.ShapeDtypeStruct((nb, NSTATE, C), F32),
        ),
        in_specs=[any_space, any_space],
        out_specs=(any_space, any_space),
        scratch_shapes=[dma((2,))],
        compiler_params=pltpu.CompilerParams(vmem_limit_bytes=4 * 1024 * 1024),
    )(on, returned)


def solution(mesh):
    in_specs = (
        P(("atm", "ocn"), None, None),
        P("ocn", None),
        P(("atm", "ocn")),
        P(("atm", "ocn"), None, None),
        P(),
        P(None, "atm", "ocn"),
        P("atm", "ocn"),
    )
    out_specs = (P(None, "atm", "ocn"), P(("atm", "ocn"), None, None))
    step = functools.partial(body, mesh.shape["atm"], mesh.shape["ocn"])
    return jax.shard_map(step, mesh=mesh, in_specs=in_specs, out_specs=out_specs, check_vma=False)
```
